256 devices in a mesh: kvp: 32 (over y, z), head: 8 (over x, core).
Axes of the slice: x: 4, y: 4, z: 8, core: 2. Of those that a mesh axis runs over, the one named last changes fastest.
Arguments:
- queries: bfloat16 [2, 128, 128], P(None, 'head'), may hold values from -200 to 200
- key_cache: bfloat16 [2, 8, 16384, 128], P(None, 'head', 'kvp'), may hold values from -6 to 6
- value_cache: bfloat16 [2, 8, 16384, 128], P(None, 'head', 'kvp'), may hold values from -6 to 6
- new_key: bfloat16 [2, 8, 128], P(None, 'head'), may hold values from -6 to 6
- new_value: bfloat16 [2, 8, 128], P(None, 'head'), may hold values from -6 to 6
- lengths: int32 [2], replicated, may hold values from 8192 to 16384, as said below
- residual_in: bfloat16 [2, 16384], P(None, ('kvp', 'head')), may hold values from -6 to 6
- out_weight: bfloat16 [16384, 16384], P('head', 'kvp'), may hold values from -0.09375 to 0.09375
- norm_gain: float32 [16384], P(('kvp', 'head')), may hold values from 0.1 to 1.9
- gate_weight: bfloat16 [26624, 16384], P(('kvp', 'head')), may hold values from -0.046875 to 0.046875
- up_weight: bfloat16 [26624, 16384], P(('kvp', 'head')), may hold values from -0.046875 to 0.046875
- down_weight: bfloat16 [26624, 16384], P(('kvp', 'head')), may hold values from -0.15625 to 0.15625
Outputs:
- layer_out: bfloat16 [2, 16384], P(None, ('kvp', 'head'))
The draws below stay inside these ranges and needn't reach their ends.
Inputs may be any that keep to these rules, and one draw needn't show every extreme that they name: `lengths`: one of the two sequences has exactly 16384 cached tokens, the other at least 8192.
All inputs are finite; a program needn't handle non-finite values.
Results may differ from the reference program's by a relative error of at most 0.017.
Values may be sent and summed in bfloat16 or wider, within the bound.
A program may use at most 64 MiB of HBM per device.

```python
import jax
import jax.numpy as jnp
from jax import lax

SEQS = 2
HQ = 128
KVH = 8
HD = 128
D = 16384
FF = 26624
CONTEXT = 16384
GROUP = 16


def cache_base(key):
    return jnp.clip(jax.random.normal(key, (SEQS, KVH, CONTEXT, HD), jnp.float32), -6.0, 6.0)


def draw_key_cache(key, part):
    base = cache_base(key)
    return base.astype(jnp.bfloat16)


def draw_queries(key, part):
    key = jax.random.fold_in(key, 13)
    return (2.5 * jnp.clip(jax.random.normal(key, (SEQS, HQ, HD), jnp.float32), -6.0, 6.0)).astype(jnp.bfloat16)


def draw_lengths(key, part):
    key = jax.random.fold_in(key, 5)
    shorter = jax.random.randint(key, (), CONTEXT // 2, CONTEXT + 1)
    chosen = jax.random.randint(jax.random.fold_in(key, 1), (), 0, 2)
    return jnp.where(jnp.arange(SEQS, dtype=jnp.int32) == chosen, CONTEXT, shorter).astype(jnp.int32)


def spiked(array, rng, source, target, parts, factor):
    def block_of(position):
        return (jnp.arange(array.shape[position]) // (array.shape[position] // parts)).reshape((-1,) + (1,) * (array.ndim - 1 - position))

    one_side = jax.random.permutation(rng, parts)[block_of(target)]
    far = (block_of(target) + parts // 2) % parts
    return jnp.where((block_of(source) == one_side) | (block_of(source) == far), factor * array, array)


def block_levels(stream_key, shape, shards, smallest, high):
    def one(dim, parts):
        steps = jax.random.uniform(jax.random.fold_in(jax.random.fold_in(stream_key, 6), dim), (parts,), jnp.float32, smallest / len(shards), high / len(shards))
        return jnp.repeat(jnp.exp(steps), shape[dim] // parts).reshape((-1,) + (1,) * (len(shape) - dim - 1))

    gain = one(*shards[0])
    for cut in shards[1:]:
        gain = gain * one(*cut)
    return gain


def noise(key, extent, scale, limit, pieces=(), kind=jnp.bfloat16):
    loudness = block_levels(key, extent, pieces, -0.22, 0.18) if pieces else 1.0
    values = jax.random.normal(key, extent, jnp.float32) * scale * loudness
    return jnp.minimum(jnp.maximum(values, -limit), limit).astype(kind)


def gaussian_with(key, extent, spread, limit, split, heavy, kind=jnp.bfloat16):
    array = spread * jax.random.normal(key, extent, jnp.float32)
    if split:
        array = array * block_levels(key, extent, split, -0.22, 0.18)
    return jnp.clip(spiked(array, jax.random.fold_in(key, 3), *heavy), -limit, limit).astype(kind)


def setup_inputs(seed: int = 0) -> dict:
    key_list = jax.random.split(jax.random.key(seed), 13)
    return {
        "queries": draw_queries(jax.random.fold_in(key_list[12], 71), 0),
        "key_cache": draw_key_cache(jax.random.fold_in(key_list[12], 71), 0),
        "value_cache": noise(key_list[2], (SEQS, KVH, CONTEXT, HD), 1.0, 6.0, ((1, 8), (2, 32))),
        "new_key": noise(key_list[3], (SEQS, KVH, HD), 1.5, 6.0, ((1, 8),)),
        "new_value": noise(key_list[4], (SEQS, KVH, HD), 1.0, 6.0, ((1, 8),)),
        "lengths": draw_lengths(jax.random.fold_in(key_list[12], 71), 0),
        "residual_in": noise(key_list[6], (SEQS, D), 1.0, 6.0, ((1, 256),)),
        "out_weight": gaussian_with(key_list[7], (HQ * HD, D), (HQ * HD) ** -0.5, 0.09375, ((0, 8), (1, 32)), (0, 1, 32, 2.75)),
        "norm_gain": jnp.clip(1.0 + 0.18 * jax.random.normal(key_list[8], (D,), jnp.float32), 0.1, 1.9),
        "gate_weight": noise(key_list[9], (FF, D), D ** -0.5, 0.046875, ((0, 256),)),
        "up_weight": noise(key_list[10], (FF, D), D ** -0.5, 0.046875, ((0, 256),)),
        "down_weight": gaussian_with(key_list[11], (FF, D), FF ** -0.5, 0.15625, ((0, 256),), (0, 1, 256, 6.0)),
    }


epsilon = 1e-05

def reference(queries, key_cache, value_cache, new_key, new_value, lengths, residual_in, out_weight, norm_gain, gate_weight, up_weight, down_weight):
    scale = 1.0 / HD ** 0.5
    grouped = queries.astype(jnp.float32).reshape(SEQS, KVH, GROUP, HD)
    scores = jnp.einsum('bghd,bgtd->bght', grouped, key_cache.astype(jnp.float32)) * scale
    positions = jnp.arange(CONTEXT, dtype=jnp.int32)
    in_range = (positions[None, :] < lengths[:, None])[:, None, None, :]
    scores = jnp.where(in_range, scores, -1e+30)
    fresh = jnp.einsum('bghd,bgd->bgh', grouped, new_key.astype(jnp.float32)) * scale
    top_score = jnp.maximum(lax.optimization_barrier(jnp.max(scores, axis=-1)), fresh)
    weights = jnp.where(in_range, jnp.exp(scores - top_score[..., None]), 0.0)
    fresh_weight = jnp.exp(fresh - top_score)
    weight_sum = lax.optimization_barrier(jnp.sum(weights, axis=-1)) + fresh_weight
    weighted = jnp.einsum('bght,bgtd->bghd', weights.astype(jnp.bfloat16).astype(jnp.float32), value_cache.astype(jnp.float32))
    weighted = weighted + fresh_weight.astype(jnp.bfloat16).astype(jnp.float32)[..., None] * new_value.astype(jnp.float32)[:, :, None, :]
    attended = (weighted / weight_sum[..., None]).astype(jnp.bfloat16).reshape(SEQS, HQ * HD)
    stream = residual_in.astype(jnp.float32) + jnp.dot(attended, out_weight, preferred_element_type=jnp.float32)
    mean_square = lax.optimization_barrier(jnp.mean(stream * stream, axis=1, keepdims=True))
    normed = (stream * jax.lax.rsqrt(mean_square + epsilon) * norm_gain[None, :]).astype(jnp.bfloat16)
    gate_act = jnp.dot(normed, gate_weight.T, preferred_element_type=jnp.float32)
    up_act = jnp.dot(normed, up_weight.T, preferred_element_type=jnp.float32)
    hidden = (jax.nn.silu(gate_act) * up_act).astype(jnp.bfloat16)
    return (stream + jnp.dot(hidden, down_weight, preferred_element_type=jnp.float32)).astype(jnp.bfloat16)
```

```python
import jax
import jax.numpy as jnp
from jax import lax
from jax.experimental import pallas as pl
from jax.experimental.pallas import tpu as pltpu
from jax.sharding import PartitionSpec as P

MESH = pl.DeviceIdType.MESH
NT = (((1,), (1,)), ((), ()))
f32 = jnp.float32
bf16 = jnp.bfloat16
EPSILON = 1e-05
MASKED = -1e30

NX, NY, NZ, NC = 4, 4, 8, 2
KVP, HEAD = NY * NZ, NX * NC
SEQS, GROUP, HD, TOKENS = 2, 16, 128, 512
D = 16384
BLOCK = D // KVP
TILES = BLOCK // 128
UNITS = 104
SCALE = HD**-0.5


def far_first(g):
    return jnp.where(lax.rem(g, 2) == 1, 4 - (g + 1) // 2, 4 + g // 2)


def kernel(
    q_ref, k_hbm, v_hbm, nk_ref, nv_ref, len_ref, res_ref, wo_hbm, gain_ref, wg_hbm, wu_hbm, wd_hbm,
    out_ref,
    k_buf, v_buf, wo_buf, wg_buf, wu_buf, wd_buf,
    y_acc, y_stat, z_acc, z_stat, att_buf,
    gain_buf, e_send, e_buf, stream_buf, f_buf, h_send, h_buf, i_send, i_buf,
    local_sem, y_send_sem, y_recv_sem, z_send_sem, z_recv_sem, ys_send_sem, ys_recv_sem, zs_send_sem, zs_recv_sem,
    gain_send_sem, gain_recv_sem, e_send_sem, e_recv_sem, f_send_sem, f_recv_sem, h_send_sem, h_recv_sem,
    i_send_sem, i_recv_sem,
):
    kvp, head = lax.axis_index("kvp"), lax.axis_index("head")
    y, z = kvp // NZ, lax.rem(kvp, NZ)
    x, core = head // NC, lax.rem(head, NC)
    slot = z * NY + y

    def at_yz(yy, zz):
        return (yy * NZ + zz, head)

    def at_head(hh):
        return (kvp, hh)

    y_peers = [(at_yz(lax.rem(y + d, NY), z)) for d in (2, 1, 3)]
    z_peers = [(at_yz(y, lax.rem(z + d, NZ))) for d in (4, 3, 5, 2, 6, 1, 7)]
    head_offsets = [(2, 1), (2, 0), (1, 1), (3, 1), (1, 0), (3, 0), (0, 1)]
    head_peers = [lax.rem(x + dx, NX) * NC + lax.rem(core + dc, NC) for dx, dc in head_offsets]

    barrier = pltpu.get_barrier_semaphore()
    greeted = z_peers + [at_head(hh) for hh in head_peers] + y_peers
    for peer in greeted:
        pl.semaphore_signal(barrier, inc=1, device_id=peer, device_id_type=MESH)

    loads = []
    for b in range(SEQS):
        loads.append(pltpu.make_async_copy(k_hbm.at[b, 0], k_buf.at[b], local_sem.at[b]))
        loads.append(pltpu.make_async_copy(v_hbm.at[b, 0], v_buf.at[b], local_sem.at[2 + b]))
    load_wo = pltpu.make_async_copy(wo_hbm, wo_buf, local_sem.at[4])
    load_wg = pltpu.make_async_copy(wg_hbm, wg_buf, local_sem.at[5])
    load_wu = pltpu.make_async_copy(wu_hbm, wu_buf, local_sem.at[6])
    load_wd = pltpu.make_async_copy(wd_hbm, wd_buf, local_sem.at[7])
    for load in loads + [load_wo, load_wg, load_wu, load_wd]:
        load.start()

    def put(src, dst, send_sem, recv_sem, peer):
        pltpu.make_async_remote_copy(
            src_ref=src, dst_ref=dst, send_sem=send_sem, recv_sem=recv_sem, device_id=peer, device_id_type=MESH
        ).start()

    def drain(ref, sem):
        pltpu.make_async_copy(ref, ref, sem).wait()

    lane = lax.broadcasted_iota(jnp.int32, (1, 128), 1)
    lane16 = lax.rem(lane, GROUP)
    lane_group = lane // GROUP
    diagonal = lax.broadcasted_iota(jnp.int32, (GROUP, 128), 0) == lax.rem(
        lax.broadcasted_iota(jnp.int32, (GROUP, 128), 1), GROUP
    )
    my_half = (lane // 64) == core

    def to_row(column):
        return jnp.sum(jnp.where(diagonal, column, 0.0), axis=0, keepdims=True)

    gain_mine = jnp.reshape(gain_ref[...], (1, 64))
    gain_buf[head] = jnp.where(my_half, jnp.concatenate([gain_mine, gain_mine], axis=1), 0.0)

    def local_attention(b):
        q = q_ref[b]
        loads[2 * b].wait()
        scores = lax.dot_general(q, k_buf[b], NT, preferred_element_type=f32) * SCALE
        positions = kvp * TOKENS + lax.broadcasted_iota(jnp.int32, (GROUP, TOKENS), 1)
        in_range = positions < len_ref[b]
        scores = jnp.where(in_range, scores, MASKED)
        first = kvp == 0
        fresh = jnp.sum(q.astype(f32) * nk_ref[b].astype(f32), axis=1, keepdims=True) * SCALE
        fresh = jnp.where(first, fresh, MASKED)
        top = jnp.maximum(jnp.max(scores, axis=1, keepdims=True), fresh)
        weights = jnp.where(in_range, jnp.exp(scores - top), 0.0)
        fresh_weight = jnp.where(first, jnp.exp(fresh - top), 0.0)
        total = jnp.sum(weights, axis=1, keepdims=True) + fresh_weight
        loads[2 * b + 1].wait()
        acc = jnp.dot(weights.astype(bf16), v_buf[b], preferred_element_type=f32)
        acc = acc + fresh_weight.astype(bf16).astype(f32) * nv_ref[b].astype(f32)
        return acc, to_row(top), to_row(total)

    def send_y(b, acc, top, total):
        y_acc[b, y] = acc.astype(bf16)
        y_stat[b, y] = jnp.concatenate([top, total], axis=0)
        for peer in y_peers:
            put(y_stat.at[b, y], y_stat.at[b, y], ys_send_sem.at[b], ys_recv_sem.at[b], peer)
            put(y_acc.at[b, y], y_acc.at[b, y], y_send_sem.at[b], y_recv_sem.at[b], peer)

    def send_z(b, acc, top, total):
        z_acc[b, z] = acc.astype(bf16)
        z_stat[b, z] = jnp.concatenate([top, total], axis=0)
        for peer in z_peers:
            put(z_stat.at[b, z], z_stat.at[b, z], zs_send_sem.at[b], zs_recv_sem.at[b], peer)
            put(z_acc.at[b, z], z_acc.at[b, z], z_send_sem.at[b], z_recv_sem.at[b], peer)

    def merge(n, b, acc_buf, stat_buf, acc_sem, stat_sem, last):
        drain(stat_buf.at[b, pl.ds(0, n - 1)], stat_sem.at[b])
        tops = [stat_buf[b, s, 0:1, :] for s in range(n)]
        totals = [stat_buf[b, s, 1:2, :] for s in range(n)]
        top = tops[0]
        for t in tops[1:]:
            top = jnp.maximum(top, t)
        total = jnp.zeros((1, 128), f32)
        chosen = jnp.zeros((1, 128), f32)
        for s in range(n):
            factor = jnp.exp(tops[s] - top)
            total = total + totals[s] * factor
            chosen = jnp.where(lane_group == s, factor, chosen)
        if last:
            chosen = chosen / total
        spread = jnp.where(diagonal, chosen, 0.0).astype(bf16)
        drain(acc_buf.at[b, pl.ds(0, n - 1)], acc_sem.at[b])
        stacked = acc_buf[b].reshape(n * GROUP, HD)
        acc = jnp.dot(spread[:, : n * GROUP], stacked, preferred_element_type=f32)
        return acc, top, total

    part0 = local_attention(0)
    part1 = local_attention(1)

    pl.semaphore_wait(barrier, len(greeted))
    send_y(0, *part0)
    send_z(1, *part1)
    for hh in head_peers:
        put(gain_buf.at[head], gain_buf.at[head], gain_send_sem, gain_recv_sem, at_head(hh))

    send_z(0, *merge(NY, 0, y_acc, y_stat, y_recv_sem, ys_recv_sem, False))
    send_y(1, *merge(NZ, 1, z_acc, z_stat, z_recv_sem, zs_recv_sem, False))
    att_buf[0] = merge(NZ, 0, z_acc, z_stat, z_recv_sem, zs_recv_sem, True)[0]
    att_buf[1] = merge(NY, 1, y_acc, y_stat, y_recv_sem, ys_recv_sem, True)[0]

    attended = jnp.concatenate([att_buf[:, h, :] for h in range(GROUP)], axis=1).astype(bf16)
    load_wo.wait()
    projected = jnp.dot(attended, wo_buf[...], preferred_element_type=f32)
    residual = res_ref[...].astype(f32)
    residual = jnp.where(my_half, jnp.concatenate([residual, residual], axis=1), 0.0)
    for t in range(TILES):
        e_buf[head, t] = projected[:, t * 128 : (t + 1) * 128] + jnp.where(x == t, residual, 0.0)
    for hh in head_peers:
        put(e_buf.at[head], e_buf.at[head], e_send_sem, e_recv_sem, at_head(hh))
    drain(gain_buf.at[pl.ds(0, HEAD - 1)], gain_recv_sem)
    gains = [gain_buf[2 * t] + gain_buf[2 * t + 1] for t in range(TILES)]
    drain(e_buf.at[pl.ds(0, HEAD - 1)], e_recv_sem)
    squares = jnp.zeros((SEQS, 128), f32)
    for t in range(TILES):
        stream = e_buf[0, t]
        for hh in range(1, HEAD):
            stream = stream + e_buf[hh, t]
        stream_buf[t] = stream
        squares = squares + stream * stream
        f_buf[slot, t] = (stream * gains[t]).astype(bf16)
    square = jnp.sum(squares, axis=1, keepdims=True)
    piece0 = square.astype(bf16).astype(f32)
    piece1 = (square - piece0).astype(bf16).astype(f32)
    piece2 = square - piece0 - piece1
    f_buf[slot, TILES] = jnp.where(
        lane == 0, piece0, jnp.where(lane == 1, piece1, jnp.where(lane == 2, piece2, 0.0))
    ).astype(bf16)

    def send_f(peer):
        put(f_buf.at[slot], f_buf.at[slot], f_send_sem, f_recv_sem.at[z], peer)

    def send_f_group(g, carry):
        zz = lax.rem(z + far_first(g), NZ)
        for dy in (2, 1, 3, 0):
            send_f(at_yz(lax.rem(y + dy, NY), zz))
        return carry

    lax.fori_loop(0, NZ - 1, send_f_group, 0)
    for dy in (2, 1, 3):
        send_f(at_yz(lax.rem(y + dy, NY), z))

    load_wg.wait()
    load_wu.wait()

    def gate_up(zz, carry):
        gate, up, squares = carry
        for yy in range(NY):
            block = zz * NY + yy
            part = jnp.concatenate([f_buf[block, t] for t in range(TILES)], axis=1)
            columns = pl.ds(pl.multiple_of((yy * NZ + zz) * BLOCK, BLOCK), BLOCK)
            gate = gate + lax.dot_general(part, wg_buf[:, columns], NT, preferred_element_type=f32)
            up = up + lax.dot_general(part, wu_buf[:, columns], NT, preferred_element_type=f32)
            squares = squares + f_buf[block, TILES].astype(f32)
        return gate, up, squares

    zero = jnp.zeros((SEQS, UNITS), f32)
    drain(f_buf.at[pl.ds(0, NY - 1)], f_recv_sem.at[z])
    carry = gate_up(z, (zero, zero, jnp.zeros((SEQS, 128), f32)))

    def gate_up_group(i, carry):
        zz = lax.rem(z + far_first(NZ - 1 - i), NZ)
        drain(f_buf.at[pl.ds(0, NY)], f_recv_sem.at[zz])
        return gate_up(zz, carry)

    gate, up, squares = lax.fori_loop(1, NZ, gate_up_group, carry)
    factor = lax.rsqrt(jnp.sum(squares, axis=1, keepdims=True) / D + EPSILON)
    gate = gate * factor
    up = up * factor
    hidden = (gate / (1.0 + jnp.exp(-gate)) * up).astype(bf16)

    load_wd.wait()

    def down(yy, zz):
        block = zz * NY + yy
        columns = pl.ds(pl.multiple_of((yy * NZ + zz) * BLOCK, BLOCK), BLOCK)
        part = jnp.dot(hidden, wd_buf[:, columns], preferred_element_type=f32).astype(bf16)
        for t in range(TILES):
            h_send[block, t] = part[:, t * 128 : (t + 1) * 128]
        return block

    def send_h(yy, zz):
        block = zz * NY + yy
        put(h_send.at[block], h_buf.at[slot], h_send_sem, h_recv_sem, at_yz(yy, zz))

    def down_group(g, carry):
        zz = lax.rem(z + far_first(g), NZ)
        for dy in (2, 1, 3, 0):
            down(lax.rem(y + dy, NY), zz)
        for dy in (2, 1, 3, 0):
            send_h(lax.rem(y + dy, NY), zz)
        return carry

    lax.fori_loop(0, NZ - 1, down_group, 0)
    for dy in (2, 1, 3):
        down(lax.rem(y + dy, NY), z)
        send_h(lax.rem(y + dy, NY), z)
    down(y, z)
    for t in range(TILES):
        h_buf[slot, t] = h_send[slot, t]
    drain(h_buf.at[pl.ds(0, KVP - 1)], h_recv_sem)

    def add_block(s, sums):
        return tuple(sums[t] + h_buf[s, t].astype(f32) for t in range(TILES))

    sums = tuple(jnp.zeros((SEQS, 128), f32) for _ in range(TILES))
    sums = lax.fori_loop(0, KVP, add_block, sums, unroll=8)
    for t in range(TILES):
        i_send[t] = sums[t]

    for (dx, dc), hh in zip(head_offsets, head_peers):
        put(i_send.at[lax.rem(x + dx, NX)], i_buf.at[head], i_send_sem, i_recv_sem, at_head(hh))
    i_buf[head] = i_send[x]
    total = stream_buf[x]
    drain(i_buf.at[pl.ds(0, HEAD - 1)], i_recv_sem)
    for hh in range(HEAD):
        total = total + i_buf[hh]
    out_ref[...] = jnp.where(core == 0, total[:, :64], total[:, 64:]).astype(bf16)

    for b in range(SEQS):
        drain(y_acc.at[b, pl.ds(0, NY - 1)], y_send_sem.at[b])
        drain(y_stat.at[b, pl.ds(0, NY - 1)], ys_send_sem.at[b])
        drain(z_acc.at[b, pl.ds(0, NZ - 1)], z_send_sem.at[b])
        drain(z_stat.at[b, pl.ds(0, NZ - 1)], zs_send_sem.at[b])
    drain(gain_buf.at[pl.ds(0, HEAD - 1)], gain_send_sem)
    drain(e_buf.at[pl.ds(0, HEAD - 1)], e_send_sem)
    drain(f_buf.at[pl.ds(0, KVP - 1)], f_send_sem)
    drain(h_buf.at[pl.ds(0, KVP - 1)], h_send_sem)
    drain(i_buf.at[pl.ds(0, HEAD - 1)], i_send_sem)


def per_device(*args):
    vmem = pl.BlockSpec(memory_space=pltpu.VMEM)
    smem = pl.BlockSpec(memory_space=pltpu.SMEM)
    hbm = pl.BlockSpec(memory_space=pl.ANY)
    dma = pltpu.SemaphoreType.DMA
    return pl.pallas_call(
        kernel,
        out_shape=jax.ShapeDtypeStruct((SEQS, D // KVP // HEAD), bf16),
        in_specs=[vmem, hbm, hbm, vmem, vmem, smem, vmem, hbm, vmem, hbm, hbm, hbm],
        out_specs=vmem,
        scratch_shapes=[
            pltpu.VMEM((SEQS, TOKENS, HD), bf16),
            pltpu.VMEM((SEQS, TOKENS, HD), bf16),
            pltpu.VMEM((GROUP * HD, BLOCK), bf16),
            pltpu.VMEM((UNITS, D), bf16),
            pltpu.VMEM((UNITS, D), bf16),
            pltpu.VMEM((UNITS, D), bf16),
            pltpu.VMEM((SEQS, NY, GROUP, HD), bf16),
            pltpu.VMEM((SEQS, NY, 2, 128), f32),
            pltpu.VMEM((SEQS, NZ, GROUP, HD), bf16),
            pltpu.VMEM((SEQS, NZ, 2, 128), f32),
            pltpu.VMEM((SEQS, GROUP, HD), f32),
            pltpu.VMEM((HEAD, 1, 128), f32),
            pltpu.VMEM((TILES, SEQS, 128), f32),
            pltpu.VMEM((HEAD, TILES, SEQS, 128), f32),
            pltpu.VMEM((TILES, SEQS, 128), f32),
            pltpu.VMEM((KVP, TILES + 1, SEQS, 128), bf16),
            pltpu.VMEM((KVP, TILES, SEQS, 128), bf16),
            pltpu.VMEM((KVP, TILES, SEQS, 128), bf16),
            pltpu.VMEM((TILES, SEQS, 128), f32),
            pltpu.VMEM((HEAD, SEQS, 128), f32),
            dma((8,)),
            dma((SEQS,)), dma((SEQS,)), dma((SEQS,)), dma((SEQS,)),
            dma((SEQS,)), dma((SEQS,)), dma((SEQS,)), dma((SEQS,)),
            dma, dma, dma, dma, dma, dma((NZ,)), dma, dma, dma, dma,
        ],
        compiler_params=pltpu.CompilerParams(
            collective_id=0, has_side_effects=True, vmem_limit_bytes=32 * 1024 * 1024
        ),
        name="layer",
    )(*args)


def solution(mesh):
    in_specs = (
        P(None, "head", None),
        P(None, "head", "kvp", None),
        P(None, "head", "kvp", None),
        P(None, "head", None),
        P(None, "head", None),
        P(),
        P(None, ("kvp", "head")),
        P("head", "kvp"),
        P(("kvp", "head")),
        P(("kvp", "head"), None),
        P(("kvp", "head"), None),
        P(("kvp", "head"), None),
    )
    return jax.shard_map(
        per_device, mesh=mesh, in_specs=in_specs, out_specs=P(None, ("kvp", "head")), check_vma=False
    )
```

```python
import jax
import jax.numpy as jnp
from jax import lax
from jax.experimental import pallas as pl
from jax.experimental.pallas import tpu as pltpu
from jax.sharding import PartitionSpec as P

MESH = pl.DeviceIdType.MESH
NT = (((1,), (1,)), ((), ()))
f32 = jnp.float32
bf16 = jnp.bfloat16
EPSILON = 1e-05
MASKED = -1e30

NX, NY, NZ, NC = 4, 4, 8, 2
KVP, HEAD = NY * NZ, NX * NC
SEQS, GROUP, HD, TOKENS = 2, 16, 128, 512
D = 16384
BLOCK = D // KVP
TILES = BLOCK // 128
UNITS = 104
SCALE = HD**-0.5


def far_first(g):
    return jnp.where(lax.rem(g, 2) == 1, 4 - (g + 1) // 2, 4 + g // 2)


def kernel(
    q_hbm, k_hbm, v_hbm, nk_hbm, nv_hbm, len_hbm, res_hbm, wo_hbm, gain_hbm, wg_hbm, wu_hbm, wd_hbm,
    out_ref,
    q_ref, nk_ref, nv_ref, len_ref, res_ref, gain_ref,
    k_buf, v_buf, wo_buf, wg_buf, wu_buf, wd_buf,
    y_acc, y_stat, z_acc, z_stat, att_buf,
    gain_buf, e_buf, stream_buf, f_buf, h_send, h_buf, i_send, i_buf,
    local_sem, y_send_sem, y_recv_sem, z_send_sem, z_recv_sem, ys_send_sem, ys_recv_sem, zs_send_sem, zs_recv_sem,
    gain_send_sem, gain_recv_sem, e_send_sem, e_recv_sem, f_send_sem, f_recv_sem, h_send_sem, h_recv_sem,
    i_send_sem, i_recv_sem, small_sem,
):
    kvp, head = lax.axis_index("kvp"), lax.axis_index("head")
    y, z = kvp // NZ, lax.rem(kvp, NZ)
    x, core = head // NC, lax.rem(head, NC)
    slot = z * NY + y

    def at_yz(yy, zz):
        return (yy * NZ + zz, head)

    def at_head(hh):
        return (kvp, hh)

    y_peers = [(at_yz(lax.rem(y + d, NY), z)) for d in (2, 1, 3)]
    z_peers = [(at_yz(y, lax.rem(z + d, NZ))) for d in (4, 3, 5, 2, 6, 1, 7)]
    head_offsets = [(2, 1), (2, 0), (1, 1), (3, 1), (1, 0), (3, 0), (0, 1)]
    head_peers = [lax.rem(x + dx, NX) * NC + lax.rem(core + dc, NC) for dx, dc in head_offsets]

    barrier = pltpu.get_barrier_semaphore()
    greeted = z_peers + [at_head(hh) for hh in head_peers] + y_peers
    for peer in greeted:
        pl.semaphore_signal(barrier, inc=1, device_id=peer, device_id_type=MESH)

    smalls = [
        pltpu.make_async_copy(src, dst, small_sem.at[i])
        for i, (src, dst) in enumerate(
            (
                (q_hbm, q_ref), (nk_hbm, nk_ref), (nv_hbm, nv_ref), (len_hbm, len_ref), (res_hbm, res_ref),
                (gain_hbm, gain_ref),
            )
        )
    ]
    loads = []
    for b in range(SEQS):
        loads.append(pltpu.make_async_copy(k_hbm.at[b, 0], k_buf.at[b], local_sem.at[b]))
        loads.append(pltpu.make_async_copy(v_hbm.at[b, 0], v_buf.at[b], local_sem.at[2 + b]))
    load_wo = pltpu.make_async_copy(wo_hbm, wo_buf, local_sem.at[4])
    load_wg = pltpu.make_async_copy(wg_hbm, wg_buf, local_sem.at[5])
    load_wu = pltpu.make_async_copy(wu_hbm, wu_buf, local_sem.at[6])
    load_wd = pltpu.make_async_copy(wd_hbm, wd_buf, local_sem.at[7])
    for load in smalls[:1] + loads + smalls[1:] + [load_wo, load_wg, load_wu, load_wd]:
        load.start()

    def put(src, dst, send_sem, recv_sem, peer):
        pltpu.make_async_remote_copy(
            src_ref=src, dst_ref=dst, send_sem=send_sem, recv_sem=recv_sem, device_id=peer, device_id_type=MESH
        ).start()

    def drain(ref, sem):
        pltpu.make_async_copy(ref, ref, sem).wait()

    lane = lax.broadcasted_iota(jnp.int32, (1, 128), 1)
    lane16 = lax.rem(lane, GROUP)
    lane_group = lane // GROUP
    diagonal = lax.broadcasted_iota(jnp.int32, (GROUP, 128), 0) == lax.rem(
        lax.broadcasted_iota(jnp.int32, (GROUP, 128), 1), GROUP
    )
    my_half = (lane // 64) == core

    def to_row(column):
        return jnp.sum(jnp.where(diagonal, column, 0.0), axis=0, keepdims=True)

    for small in smalls:
        small.wait()

    gain_mine = jnp.reshape(gain_ref[...], (1, 64))
    gain_buf[head] = jnp.where(my_half, jnp.concatenate([gain_mine, gain_mine], axis=1), 0.0)

    def local_attention(b):
        q = q_ref[b]
        loads[2 * b].wait()
        scores = lax.dot_general(q, k_buf[b], NT, preferred_element_type=f32) * SCALE
        positions = kvp * TOKENS + lax.broadcasted_iota(jnp.int32, (GROUP, TOKENS), 1)
        in_range = positions < len_ref[b]
        scores = jnp.where(in_range, scores, MASKED)
        first = kvp == 0
        fresh = jnp.sum(q.astype(f32) * nk_ref[b : b + 1, :].astype(f32), axis=1, keepdims=True) * SCALE
        fresh = jnp.where(first, fresh, MASKED)
        top = jnp.maximum(jnp.max(scores, axis=1, keepdims=True), fresh)
        weights = jnp.where(in_range, jnp.exp(scores - top), 0.0)
        fresh_weight = jnp.where(first, jnp.exp(fresh - top), 0.0)
        total = jnp.sum(weights, axis=1, keepdims=True) + fresh_weight
        loads[2 * b + 1].wait()
        acc = jnp.dot(weights.astype(bf16), v_buf[b], preferred_element_type=f32)
        acc = acc + fresh_weight.astype(bf16).astype(f32) * nv_ref[b : b + 1, :].astype(f32)
        return acc, to_row(top), to_row(total)

    def send_y(b, acc, top, total):
        y_acc[b, y] = acc.astype(bf16)
        y_stat[b, y] = jnp.concatenate([top, total], axis=0)
        for peer in y_peers:
            put(y_stat.at[b, y], y_stat.at[b, y], ys_send_sem.at[b], ys_recv_sem.at[b], peer)
            put(y_acc.at[b, y], y_acc.at[b, y], y_send_sem.at[b], y_recv_sem.at[b], peer)

    def send_z(b, acc, top, total):
        z_acc[b, z] = acc.astype(bf16)
        z_stat[b, z] = jnp.concatenate([top, total], axis=0)
        for peer in z_peers:
            put(z_stat.at[b, z], z_stat.at[b, z], zs_send_sem.at[b], zs_recv_sem.at[b], peer)
            put(z_acc.at[b, z], z_acc.at[b, z], z_send_sem.at[b], z_recv_sem.at[b], peer)

    def merge(n, b, acc_buf, stat_buf, acc_sem, stat_sem, last):
        drain(stat_buf.at[b, pl.ds(0, n - 1)], stat_sem.at[b])
        tops = [stat_buf[b, s, 0:1, :] for s in range(n)]
        totals = [stat_buf[b, s, 1:2, :] for s in range(n)]
        top = tops[0]
        for t in tops[1:]:
            top = jnp.maximum(top, t)
        total = jnp.zeros((1, 128), f32)
        chosen = jnp.zeros((1, 128), f32)
        for s in range(n):
            factor = jnp.exp(tops[s] - top)
            total = total + totals[s] * factor
            chosen = jnp.where(lane_group == s, factor, chosen)
        if last:
            chosen = chosen / total
        spread = jnp.where(diagonal, chosen, 0.0).astype(bf16)
        drain(acc_buf.at[b, pl.ds(0, n - 1)], acc_sem.at[b])
        stacked = acc_buf[b].reshape(n * GROUP, HD)
        acc = jnp.dot(spread[:, : n * GROUP], stacked, preferred_element_type=f32)
        return acc, top, total

    part0 = local_attention(0)
    part1 = local_attention(1)

    pl.semaphore_wait(barrier, len(greeted))
    send_y(0, *part0)
    send_z(1, *part1)
    for hh in head_peers:
        put(gain_buf.at[head], gain_buf.at[head], gain_send_sem, gain_recv_sem, at_head(hh))

    send_z(0, *merge(NY, 0, y_acc, y_stat, y_recv_sem, ys_recv_sem, False))
    send_y(1, *merge(NZ, 1, z_acc, z_stat, z_recv_sem, zs_recv_sem, False))
    att_buf[0] = merge(NZ, 0, z_acc, z_stat, z_recv_sem, zs_recv_sem, True)[0]
    att_buf[1] = merge(NY, 1, y_acc, y_stat, y_recv_sem, ys_recv_sem, True)[0]

    attended = jnp.concatenate([att_buf[:, h, :] for h in range(GROUP)], axis=1).astype(bf16)
    load_wo.wait()
    projected = jnp.dot(attended, wo_buf[...], preferred_element_type=f32)
    residual = res_ref[...].astype(f32)
    residual = jnp.where(my_half, jnp.concatenate([residual, residual], axis=1), 0.0)
    for t in range(TILES):
        e_buf[head, t] = projected[:, t * 128 : (t + 1) * 128] + jnp.where(x == t, residual, 0.0)
    for hh in head_peers:
        put(e_buf.at[head], e_buf.at[head], e_send_sem, e_recv_sem, at_head(hh))
    drain(gain_buf.at[pl.ds(0, HEAD - 1)], gain_recv_sem)
    gains = [gain_buf[2 * t] + gain_buf[2 * t + 1] for t in range(TILES)]
    drain(e_buf.at[pl.ds(0, HEAD - 1)], e_recv_sem)
    squares = jnp.zeros((SEQS, 128), f32)
    for t in range(TILES):
        stream = e_buf[0, t]
        for hh in range(1, HEAD):
            stream = stream + e_buf[hh, t]
        stream_buf[t] = stream
        squares = squares + stream * stream
        f_buf[slot, t] = (stream * gains[t]).astype(bf16)
    square = jnp.sum(squares, axis=1, keepdims=True)
    piece0 = square.astype(bf16).astype(f32)
    piece1 = (square - piece0).astype(bf16).astype(f32)
    piece2 = square - piece0 - piece1
    f_buf[slot, TILES] = jnp.where(
        lane == 0, piece0, jnp.where(lane == 1, piece1, jnp.where(lane == 2, piece2, 0.0))
    ).astype(bf16)

    def send_f(peer):
        put(f_buf.at[slot], f_buf.at[slot], f_send_sem, f_recv_sem.at[z], peer)

    def send_f_group(g, carry):
        zz = lax.rem(z + far_first(g), NZ)
        for dy in (2, 1, 3, 0):
            send_f(at_yz(lax.rem(y + dy, NY), zz))
        return carry

    lax.fori_loop(0, NZ - 1, send_f_group, 0)
    for dy in (2, 1, 3):
        send_f(at_yz(lax.rem(y + dy, NY), z))

    load_wg.wait()
    load_wu.wait()

    def gate_up(zz, carry):
        gate, up, squares = carry
        for yy in range(NY):
            block = zz * NY + yy
            part = jnp.concatenate([f_buf[block, t] for t in range(TILES)], axis=1)
            columns = pl.ds(pl.multiple_of((yy * NZ + zz) * BLOCK, BLOCK), BLOCK)
            gate = gate + lax.dot_general(part, wg_buf[:, columns], NT, preferred_element_type=f32)
            up = up + lax.dot_general(part, wu_buf[:, columns], NT, preferred_element_type=f32)
            squares = squares + f_buf[block, TILES].astype(f32)
        return gate, up, squares

    zero = jnp.zeros((SEQS, UNITS), f32)
    drain(f_buf.at[pl.ds(0, NY - 1)], f_recv_sem.at[z])
    carry = gate_up(z, (zero, zero, jnp.zeros((SEQS, 128), f32)))

    def gate_up_group(i, carry):
        zz = lax.rem(z + far_first(NZ - 1 - i), NZ)
        drain(f_buf.at[pl.ds(0, NY)], f_recv_sem.at[zz])
        return gate_up(zz, carry)

    gate, up, squares = lax.fori_loop(1, NZ, gate_up_group, carry)
    factor = lax.rsqrt(jnp.sum(squares, axis=1, keepdims=True) / D + EPSILON)
    gate = gate * factor
    up = up * factor
    hidden = (gate / (1.0 + jnp.exp(-gate)) * up).astype(bf16)

    load_wd.wait()

    def down(yy, zz):
        block = zz * NY + yy
        columns = pl.ds(pl.multiple_of((yy * NZ + zz) * BLOCK, BLOCK), BLOCK)
        part = jnp.dot(hidden, wd_buf[:, columns], preferred_element_type=f32).astype(bf16)
        for t in range(TILES):
            h_send[block, t] = part[:, t * 128 : (t + 1) * 128]
        return block

    def send_h(yy, zz):
        block = zz * NY + yy
        put(h_send.at[block], h_buf.at[slot], h_send_sem, h_recv_sem, at_yz(yy, zz))

    def down_group(g, carry):
        zz = lax.rem(z + far_first(g), NZ)
        for dy in (2, 1, 3, 0):
            down(lax.rem(y + dy, NY), zz)
        for dy in (2, 1, 3, 0):
            send_h(lax.rem(y + dy, NY), zz)
        return carry

    lax.fori_loop(0, NZ - 1, down_group, 0)
    for dy in (2, 1, 3):
        down(lax.rem(y + dy, NY), z)
        send_h(lax.rem(y + dy, NY), z)
    down(y, z)
    for t in range(TILES):
        h_buf[slot, t] = h_send[slot, t]
    drain(h_buf.at[pl.ds(0, KVP - 1)], h_recv_sem)

    def add_block(s, sums):
        return tuple(sums[t] + h_buf[s, t].astype(f32) for t in range(TILES))

    sums = tuple(jnp.zeros((SEQS, 128), f32) for _ in range(TILES))
    sums = lax.fori_loop(0, KVP, add_block, sums, unroll=8)
    for t in range(TILES):
        i_send[t] = sums[t]

    for (dx, dc), hh in zip(head_offsets, head_peers):
        put(i_send.at[lax.rem(x + dx, NX)], i_buf.at[head], i_send_sem, i_recv_sem, at_head(hh))
    i_buf[head] = i_send[x]
    total = stream_buf[x]
    drain(i_buf.at[pl.ds(0, HEAD - 1)], i_recv_sem)
    for hh in range(HEAD):
        total = total + i_buf[hh]
    out_ref[...] = jnp.where(core == 0, total[:, :64], total[:, 64:]).astype(bf16)

    for b in range(SEQS):
        drain(y_acc.at[b, pl.ds(0, NY - 1)], y_send_sem.at[b])
        drain(y_stat.at[b, pl.ds(0, NY - 1)], ys_send_sem.at[b])
        drain(z_acc.at[b, pl.ds(0, NZ - 1)], z_send_sem.at[b])
        drain(z_stat.at[b, pl.ds(0, NZ - 1)], zs_send_sem.at[b])
    drain(gain_buf.at[pl.ds(0, HEAD - 1)], gain_send_sem)
    drain(e_buf.at[pl.ds(0, HEAD - 1)], e_send_sem)
    drain(f_buf.at[pl.ds(0, KVP - 1)], f_send_sem)
    drain(h_buf.at[pl.ds(0, KVP - 1)], h_send_sem)
    drain(i_buf.at[pl.ds(0, HEAD - 1)], i_send_sem)


def per_device(queries, key_cache, value_cache, new_key, new_value, *rest):
    args = (queries, key_cache, value_cache, new_key.reshape(SEQS, HD), new_value.reshape(SEQS, HD)) + rest
    vmem = pl.BlockSpec(memory_space=pltpu.VMEM)
    hbm = pl.BlockSpec(memory_space=pltpu.HBM)
    dma = pltpu.SemaphoreType.DMA
    return pl.pallas_call(
        kernel,
        out_shape=jax.ShapeDtypeStruct((SEQS, D // KVP // HEAD), bf16),
        in_specs=[hbm] * 12,
        out_specs=vmem,
        scratch_shapes=[
            pltpu.VMEM((SEQS, GROUP, HD), bf16),
            pltpu.VMEM((SEQS, HD), bf16),
            pltpu.VMEM((SEQS, HD), bf16),
            pltpu.SMEM((SEQS,), jnp.int32),
            pltpu.VMEM((SEQS, D // KVP // HEAD), bf16),
            pltpu.VMEM((D // KVP // HEAD,), f32),
            pltpu.VMEM((SEQS, TOKENS, HD), bf16),
            pltpu.VMEM((SEQS, TOKENS, HD), bf16),
            pltpu.VMEM((GROUP * HD, BLOCK), bf16),
            pltpu.VMEM((UNITS, D), bf16),
            pltpu.VMEM((UNITS, D), bf16),
            pltpu.VMEM((UNITS, D), bf16),
            pltpu.VMEM((SEQS, NY, GROUP, HD), bf16),
            pltpu.VMEM((SEQS, NY, 2, 128), f32),
            pltpu.VMEM((SEQS, NZ, GROUP, HD), bf16),
            pltpu.VMEM((SEQS, NZ, 2, 128), f32),
            pltpu.VMEM((SEQS, GROUP, HD), f32),
            pltpu.VMEM((HEAD, 1, 128), f32),
            pltpu.VMEM((HEAD, TILES, SEQS, 128), f32),
            pltpu.VMEM((TILES, SEQS, 128), f32),
            pltpu.VMEM((KVP, TILES + 1, SEQS, 128), bf16),
            pltpu.VMEM((KVP, TILES, SEQS, 128), bf16),
            pltpu.VMEM((KVP, TILES, SEQS, 128), bf16),
            pltpu.VMEM((TILES, SEQS, 128), f32),
            pltpu.VMEM((HEAD, SEQS, 128), f32),
            dma((8,)),
            dma((SEQS,)), dma((SEQS,)), dma((SEQS,)), dma((SEQS,)),
            dma((SEQS,)), dma((SEQS,)), dma((SEQS,)), dma((SEQS,)),
            dma, dma, dma, dma, dma, dma((NZ,)), dma, dma, dma, dma, dma((6,)),
        ],
        compiler_params=pltpu.CompilerParams(
            collective_id=0, has_side_effects=True, vmem_limit_bytes=64 * 1024 * 1024
        ),
        name="layer",
    )(*args)


def solution(mesh):
    in_specs = (
        P(None, "head", None),
        P(None, "head", "kvp", None),
        P(None, "head", "kvp", None),
        P(None, "head", None),
        P(None, "head", None),
        P(),
        P(None, ("kvp", "head")),
        P("head", "kvp"),
        P(("kvp", "head")),
        P(("kvp", "head"), None),
        P(("kvp", "head"), None),
        P(("kvp", "head"), None),
    )
    return jax.shard_map(
        per_device, mesh=mesh, in_specs=in_specs, out_specs=P(None, ("kvp", "head")), check_vma=False
    )
```

```python
import jax
import jax.numpy as jnp
from jax import lax
from jax.experimental import pallas as pl
from jax.experimental.pallas import tpu as pltpu
from jax.sharding import PartitionSpec as P

MESH = pl.DeviceIdType.MESH
NT = (((1,), (1,)), ((), ()))
f32 = jnp.float32
bf16 = jnp.bfloat16
EPSILON = 1e-05
MASKED = -1e30

NX, NY, NZ, NC = 4, 4, 8, 2
KVP, HEAD = NY * NZ, NX * NC
SEQS, GROUP, HD, TOKENS = 2, 16, 128, 512
D = 16384
BLOCK = D // KVP
TILES = BLOCK // 128
UNITS = 104
SCALE = HD**-0.5


def far_first(g):
    return jnp.where(lax.rem(g, 2) == 1, 4 - (g + 1) // 2, 4 + g // 2)


def kernel(
    q_hbm, k_hbm, v_hbm, nk_hbm, nv_hbm, len_hbm, res_hbm, wo_hbm, gain_hbm, wg_hbm, wu_hbm, wd_hbm,
    out_ref,
    q_ref, nk_ref, nv_ref, len_ref, res_ref, gain_ref,
    k_buf, v_buf, wo_buf, wgu_buf, wd_buf,
    y_acc, y_stat, z_acc, z_stat, att_buf,
    gain_buf, e_buf, stream_buf, f_buf, h_send, h_buf, i_send, i_buf,
    local_sem, y_send_sem, y_recv_sem, z_send_sem, z_recv_sem, ys_send_sem, ys_recv_sem, zs_send_sem, zs_recv_sem,
    gain_send_sem, gain_recv_sem, e_send_sem, e_recv_sem, f_send_sem, f_recv_sem, h_send_sem, h_recv_sem,
    i_send_sem, i_recv_sem, small_sem,
):
    kvp, head = lax.axis_index("kvp"), lax.axis_index("head")
    y, z = kvp // NZ, lax.rem(kvp, NZ)
    x, core = head // NC, lax.rem(head, NC)
    slot = z * NY + y

    def at_yz(yy, zz):
        return (yy * NZ + zz, head)

    def at_head(hh):
        return (kvp, hh)

    y_peers = [(at_yz(lax.rem(y + d, NY), z)) for d in (2, 1, 3)]
    z_peers = [(at_yz(y, lax.rem(z + d, NZ))) for d in (4, 3, 5, 2, 6, 1, 7)]
    head_offsets = [(2, 1), (2, 0), (1, 1), (3, 1), (1, 0), (3, 0), (0, 1)]
    head_peers = [lax.rem(x + dx, NX) * NC + lax.rem(core + dc, NC) for dx, dc in head_offsets]

    smalls = [
        pltpu.make_async_copy(src, dst, small_sem.at[i])
        for i, (src, dst) in enumerate(
            (
                (q_hbm, q_ref), (nk_hbm, nk_ref), (nv_hbm, nv_ref), (len_hbm, len_ref), (res_hbm, res_ref),
                (gain_hbm, gain_ref),
            )
        )
    ]
    loads = []
    for b in range(SEQS):
        loads.append(pltpu.make_async_copy(k_hbm.at[b, 0], k_buf.at[b], local_sem.at[b]))
        loads.append(pltpu.make_async_copy(v_hbm.at[b, 0], v_buf.at[b], local_sem.at[2 + b]))
    load_wo = pltpu.make_async_copy(wo_hbm, wo_buf, local_sem.at[4])
    load_wg = pltpu.make_async_copy(wg_hbm, wgu_buf.at[pl.ds(0, UNITS)], local_sem.at[5])
    load_wu = pltpu.make_async_copy(wu_hbm, wgu_buf.at[pl.ds(128, UNITS)], local_sem.at[6])
    load_wd = pltpu.make_async_copy(wd_hbm, wd_buf, local_sem.at[7])
    for load in smalls[:1] + loads + smalls[1:]:
        load.start()

    barrier = pltpu.get_barrier_semaphore()
    greeted = z_peers + [at_head(hh) for hh in head_peers] + y_peers
    for peer in greeted:
        pl.semaphore_signal(barrier, inc=1, device_id=peer, device_id_type=MESH)

    def put(src, dst, send_sem, recv_sem, peer):
        pltpu.make_async_remote_copy(
            src_ref=src, dst_ref=dst, send_sem=send_sem, recv_sem=recv_sem, device_id=peer, device_id_type=MESH
        ).start()

    def drain(ref, sem):
        pltpu.make_async_copy(ref, ref, sem).wait()

    lane = lax.broadcasted_iota(jnp.int32, (1, 128), 1)
    lane16 = lax.rem(lane, GROUP)
    lane_group = lane // GROUP
    diagonal = lax.broadcasted_iota(jnp.int32, (GROUP, 128), 0) == lax.rem(
        lax.broadcasted_iota(jnp.int32, (GROUP, 128), 1), GROUP
    )
    my_half = (lane // 64) == core

    def to_row(column):
        return jnp.sum(jnp.where(diagonal, column, 0.0), axis=0, keepdims=True)

    for small in smalls + loads:
        small.wait()
    for load in (load_wo, load_wg, load_wu, load_wd):
        load.start()

    gain_mine = jnp.reshape(gain_ref[...], (1, 64))
    gain_buf[head] = jnp.where(my_half, jnp.concatenate([gain_mine, gain_mine], axis=1), 0.0)

    def local_attention(b):
        q = q_ref[b]
        scores = lax.dot_general(q, k_buf[b], NT, preferred_element_type=f32) * SCALE
        positions = kvp * TOKENS + lax.broadcasted_iota(jnp.int32, (GROUP, TOKENS), 1)
        in_range = positions < len_ref[b]
        scores = jnp.where(in_range, scores, MASKED)
        first = kvp == 0
        fresh = jnp.sum(q.astype(f32) * nk_ref[b : b + 1, :].astype(f32), axis=1, keepdims=True) * SCALE
        fresh = jnp.where(first, fresh, MASKED)
        top = jnp.maximum(jnp.max(scores, axis=1, keepdims=True), fresh)
        weights = jnp.where(in_range, jnp.exp(scores - top), 0.0)
        fresh_weight = jnp.where(first, jnp.exp(fresh - top), 0.0)
        total = jnp.sum(weights, axis=1, keepdims=True) + fresh_weight
        acc = jnp.dot(weights.astype(bf16), v_buf[b], preferred_element_type=f32)
        acc = acc + fresh_weight.astype(bf16).astype(f32) * nv_ref[b : b + 1, :].astype(f32)
        return acc, to_row(top), to_row(total)

    def send_y(b, acc, top, total):
        y_acc[b, y] = acc.astype(bf16)
        y_stat[b, y] = jnp.concatenate([top, total], axis=0)
        for peer in y_peers:
            put(y_stat.at[b, y], y_stat.at[b, y], ys_send_sem.at[b], ys_recv_sem.at[b], peer)
            put(y_acc.at[b, y], y_acc.at[b, y], y_send_sem.at[b], y_recv_sem.at[b], peer)

    def send_z(b, acc, top, total):
        z_acc[b, z] = acc.astype(bf16)
        z_stat[b, z] = jnp.concatenate([top, total], axis=0)
        for peer in z_peers:
            put(z_stat.at[b, z], z_stat.at[b, z], zs_send_sem.at[b], zs_recv_sem.at[b], peer)
            put(z_acc.at[b, z], z_acc.at[b, z], z_send_sem.at[b], z_recv_sem.at[b], peer)

    def merge(n, b, acc_buf, stat_buf, acc_sem, stat_sem, last):
        drain(stat_buf.at[b, pl.ds(0, n - 1)], stat_sem.at[b])
        tops = [stat_buf[b, s, 0:1, :] for s in range(n)]
        totals = [stat_buf[b, s, 1:2, :] for s in range(n)]
        top = tops[0]
        for t in tops[1:]:
            top = jnp.maximum(top, t)
        total = jnp.zeros((1, 128), f32)
        chosen = jnp.zeros((1, 128), f32)
        for s in range(n):
            factor = jnp.exp(tops[s] - top)
            total = total + totals[s] * factor
            chosen = jnp.where(lane_group == s, factor, chosen)
        if last:
            chosen = chosen / total
        spread = jnp.where(diagonal, chosen, 0.0).astype(bf16)
        drain(acc_buf.at[b, pl.ds(0, n - 1)], acc_sem.at[b])
        stacked = acc_buf[b].reshape(n * GROUP, HD)
        acc = jnp.dot(spread[:, : n * GROUP], stacked, preferred_element_type=f32)
        return acc, top, total

    part0 = local_attention(0)
    part1 = local_attention(1)

    pl.semaphore_wait(barrier, len(greeted))
    send_y(0, *part0)
    send_z(1, *part1)
    for hh in head_peers:
        put(gain_buf.at[head], gain_buf.at[head], gain_send_sem, gain_recv_sem, at_head(hh))

    send_z(0, *merge(NY, 0, y_acc, y_stat, y_recv_sem, ys_recv_sem, False))
    send_y(1, *merge(NZ, 1, z_acc, z_stat, z_recv_sem, zs_recv_sem, False))
    att_buf[0] = merge(NZ, 0, z_acc, z_stat, z_recv_sem, zs_recv_sem, True)[0]
    att_buf[1] = merge(NY, 1, y_acc, y_stat, y_recv_sem, ys_recv_sem, True)[0]

    attended = jnp.concatenate([att_buf[:, h, :] for h in range(GROUP)], axis=1).astype(bf16)
    load_wo.wait()
    projected = jnp.dot(attended, wo_buf[...], preferred_element_type=f32)
    residual = res_ref[...].astype(f32)
    residual = jnp.where(my_half, jnp.concatenate([residual, residual], axis=1), 0.0)
    for t in range(TILES):
        e_buf[head, t] = projected[:, t * 128 : (t + 1) * 128] + jnp.where(x == t, residual, 0.0)
    for hh in head_peers:
        put(e_buf.at[head], e_buf.at[head], e_send_sem, e_recv_sem, at_head(hh))
    drain(gain_buf.at[pl.ds(0, HEAD - 1)], gain_recv_sem)
    gains = [gain_buf[2 * t] + gain_buf[2 * t + 1] for t in range(TILES)]
    drain(e_buf.at[pl.ds(0, HEAD - 1)], e_recv_sem)
    squares = jnp.zeros((SEQS, 128), f32)
    for t in range(TILES):
        stream = e_buf[0, t]
        for hh in range(1, HEAD):
            stream = stream + e_buf[hh, t]
        stream_buf[t] = stream
        squares = squares + stream * stream
        f_buf[slot, t] = (stream * gains[t]).astype(bf16)
    square = jnp.sum(squares, axis=1, keepdims=True)
    piece0 = square.astype(bf16).astype(f32)
    piece1 = (square - piece0).astype(bf16).astype(f32)
    piece2 = square - piece0 - piece1
    f_buf[slot, TILES] = jnp.where(
        lane == 0, piece0, jnp.where(lane == 1, piece1, jnp.where(lane == 2, piece2, 0.0))
    ).astype(bf16)

    def send_f(peer):
        put(f_buf.at[slot], f_buf.at[slot], f_send_sem, f_recv_sem.at[z], peer)

    def send_f_group(g, carry):
        zz = lax.rem(z + far_first(g), NZ)
        for dy in (2, 1, 3, 0):
            send_f(at_yz(lax.rem(y + dy, NY), zz))
        return carry

    lax.fori_loop(0, NZ - 1, send_f_group, 0)
    for dy in (2, 1, 3):
        send_f(at_yz(lax.rem(y + dy, NY), z))

    load_wg.wait()
    load_wu.wait()

    def gate_up(zz, carry):
        acts, squares = carry
        for yy in range(NY):
            block = zz * NY + yy
            part = jnp.concatenate([f_buf[block, t] for t in range(TILES)], axis=1)
            columns = pl.ds(pl.multiple_of((yy * NZ + zz) * BLOCK, BLOCK), BLOCK)
            acts = acts + lax.dot_general(part, wgu_buf[:, columns], NT, preferred_element_type=f32)
            squares = squares + f_buf[block, TILES].astype(f32)
        return acts, squares

    drain(f_buf.at[pl.ds(0, NY - 1)], f_recv_sem.at[z])
    carry = gate_up(z, (jnp.zeros((SEQS, 256), f32), jnp.zeros((SEQS, 128), f32)))

    def gate_up_group(i, carry):
        zz = lax.rem(z + far_first(NZ - 1 - i), NZ)
        drain(f_buf.at[pl.ds(0, NY)], f_recv_sem.at[zz])
        return gate_up(zz, carry)

    acts, squares = lax.fori_loop(1, NZ, gate_up_group, carry)
    factor = lax.rsqrt(jnp.sum(squares, axis=1, keepdims=True) / D + EPSILON)
    gate = acts[:, :UNITS] * factor
    up = acts[:, 128 : 128 + UNITS] * factor
    hidden = (gate / (1.0 + jnp.exp(-gate)) * up).astype(bf16)

    load_wd.wait()

    def down(yy, zz):
        block = zz * NY + yy
        columns = pl.ds(pl.multiple_of((yy * NZ + zz) * BLOCK, BLOCK), BLOCK)
        part = jnp.dot(hidden, wd_buf[:, columns], preferred_element_type=f32).astype(bf16)
        for t in range(TILES):
            h_send[block, t] = part[:, t * 128 : (t + 1) * 128]
        return block

    def send_h(yy, zz):
        block = zz * NY + yy
        put(h_send.at[block], h_buf.at[slot], h_send_sem, h_recv_sem.at[z], at_yz(yy, zz))

    def down_group(g, carry):
        zz = lax.rem(z + far_first(g), NZ)
        for dy in (2, 1, 3, 0):
            down(lax.rem(y + dy, NY), zz)
        for dy in (2, 1, 3, 0):
            send_h(lax.rem(y + dy, NY), zz)
        return carry

    lax.fori_loop(0, NZ - 1, down_group, 0)
    for dy in (2, 1, 3):
        down(lax.rem(y + dy, NY), z)
        send_h(lax.rem(y + dy, NY), z)
    down(y, z)
    for t in range(TILES):
        h_buf[slot, t] = h_send[slot, t]

    def add_blocks(zz, sums):
        for yy in range(NY):
            sums = tuple(sums[t] + h_buf[zz * NY + yy, t].astype(f32) for t in range(TILES))
        return sums

    def add_group(i, sums):
        zz = lax.rem(z + far_first(NZ - 1 - i), NZ)
        drain(h_buf.at[pl.ds(0, NY)], h_recv_sem.at[zz])
        return add_blocks(zz, sums)

    drain(h_buf.at[pl.ds(0, NY - 1)], h_recv_sem.at[z])
    sums = add_blocks(z, tuple(jnp.zeros((SEQS, 128), f32) for _ in range(TILES)))
    sums = lax.fori_loop(1, NZ, add_group, sums)
    for t in range(TILES):
        i_send[t] = sums[t]

    for (dx, dc), hh in zip(head_offsets, head_peers):
        put(i_send.at[lax.rem(x + dx, NX)], i_buf.at[head], i_send_sem, i_recv_sem, at_head(hh))
    i_buf[head] = i_send[x]
    total = stream_buf[x]
    drain(i_buf.at[pl.ds(0, HEAD - 1)], i_recv_sem)
    for hh in range(HEAD):
        total = total + i_buf[hh]
    out_ref[...] = jnp.where(core == 0, total[:, :64], total[:, 64:]).astype(bf16)

    for b in range(SEQS):
        drain(y_acc.at[b, pl.ds(0, NY - 1)], y_send_sem.at[b])
        drain(y_stat.at[b, pl.ds(0, NY - 1)], ys_send_sem.at[b])
        drain(z_acc.at[b, pl.ds(0, NZ - 1)], z_send_sem.at[b])
        drain(z_stat.at[b, pl.ds(0, NZ - 1)], zs_send_sem.at[b])
    drain(gain_buf.at[pl.ds(0, HEAD - 1)], gain_send_sem)
    drain(e_buf.at[pl.ds(0, HEAD - 1)], e_send_sem)
    drain(f_buf.at[pl.ds(0, KVP - 1)], f_send_sem)
    drain(h_buf.at[pl.ds(0, KVP - 1)], h_send_sem)
    drain(i_buf.at[pl.ds(0, HEAD - 1)], i_send_sem)


def per_device(queries, key_cache, value_cache, new_key, new_value, *rest):
    args = (queries, key_cache, value_cache, new_key.reshape(SEQS, HD), new_value.reshape(SEQS, HD)) + rest
    vmem = pl.BlockSpec(memory_space=pltpu.VMEM)
    hbm = pl.BlockSpec(memory_space=pltpu.HBM)
    dma = pltpu.SemaphoreType.DMA
    return pl.pallas_call(
        kernel,
        out_shape=pltpu.VMEM((SEQS, D // KVP // HEAD), bf16),
        in_specs=[hbm] * 12,
        out_specs=vmem,
        scratch_shapes=[
            pltpu.VMEM((SEQS, GROUP, HD), bf16),
            pltpu.VMEM((SEQS, HD), bf16),
            pltpu.VMEM((SEQS, HD), bf16),
            pltpu.SMEM((SEQS,), jnp.int32),
            pltpu.VMEM((SEQS, D // KVP // HEAD), bf16),
            pltpu.VMEM((D // KVP // HEAD,), f32),
            pltpu.VMEM((SEQS, TOKENS, HD), bf16),
            pltpu.VMEM((SEQS, TOKENS, HD), bf16),
            pltpu.VMEM((GROUP * HD, BLOCK), bf16),
            pltpu.VMEM((256, D), bf16),
            pltpu.VMEM((UNITS, D), bf16),
            pltpu.VMEM((SEQS, NY, GROUP, HD), bf16),
            pltpu.VMEM((SEQS, NY, 2, 128), f32),
            pltpu.VMEM((SEQS, NZ, GROUP, HD), bf16),
            pltpu.VMEM((SEQS, NZ, 2, 128), f32),
            pltpu.VMEM((SEQS, GROUP, HD), f32),
            pltpu.VMEM((HEAD, 1, 128), f32),
            pltpu.VMEM((HEAD, TILES, SEQS, 128), f32),
            pltpu.VMEM((TILES, SEQS, 128), f32),
            pltpu.VMEM((KVP, TILES + 1, SEQS, 128), bf16),
            pltpu.VMEM((KVP, TILES, SEQS, 128), bf16),
            pltpu.VMEM((KVP, TILES, SEQS, 128), bf16),
            pltpu.VMEM((TILES, SEQS, 128), f32),
            pltpu.VMEM((HEAD, SEQS, 128), f32),
            dma((8,)),
            dma((SEQS,)), dma((SEQS,)), dma((SEQS,)), dma((SEQS,)),
            dma((SEQS,)), dma((SEQS,)), dma((SEQS,)), dma((SEQS,)),
            dma, dma, dma, dma, dma, dma((NZ,)), dma, dma((NZ,)), dma, dma, dma((6,)),
        ],
        compiler_params=pltpu.CompilerParams(
            collective_id=0, has_side_effects=True, vmem_limit_bytes=62 * 1024 * 1024
        ),
        name="layer",
    )(*args)


def solution(mesh):
    in_specs = (
        P(None, "head", None),
        P(None, "head", "kvp", None),
        P(None, "head", "kvp", None),
        P(None, "head", None),
        P(None, "head", None),
        P(),
        P(None, ("kvp", "head")),
        P("head", "kvp"),
        P(("kvp", "head")),
        P(("kvp", "head"), None),
        P(("kvp", "head"), None),
        P(("kvp", "head"), None),
    )
    return jax.shard_map(
        per_device, mesh=mesh, in_specs=in_specs, out_specs=P(None, ("kvp", "head")), check_vma=False
    )
```

```python
import jax
import jax.numpy as jnp
from jax import lax
from jax.experimental import pallas as pl
from jax.experimental.pallas import tpu as pltpu
from jax.sharding import PartitionSpec as P

MESH = pl.DeviceIdType.MESH
NT = (((1,), (1,)), ((), ()))
f32 = jnp.float32
bf16 = jnp.bfloat16
EPSILON = 1e-05
MASKED = -1e30

NX, NY, NZ, NC = 4, 4, 8, 2
KVP, HEAD = NY * NZ, NX * NC
SEQS, GROUP, HD, TOKENS = 2, 16, 128, 512
D = 16384
BLOCK = D // KVP
TILES = BLOCK // 128
UNITS = 104
SCALE = HD**-0.5


def far_first(g):
    return jnp.where(lax.rem(g, 2) == 1, 4 - (g + 1) // 2, 4 + g // 2)


def packed(offsets):
    return sum(offset << (3 * i) for i, offset in enumerate(offsets))


SENT, USED = packed((4, 1, 7, 2, 6, 3, 5)), packed((1, 7, 0, 2, 6, 4, 3, 5))


def nth(offsets, i):
    return jnp.bitwise_and(lax.shift_right_logical(jnp.int32(offsets), jnp.int32(3 * i)), 7)


def kernel(
    q_hbm, k_hbm, v_hbm, nk_hbm, nv_hbm, len_hbm, res_hbm, wo_hbm, gain_hbm, wg_hbm, wu_hbm, wd_hbm,
    out_ref,
    q_ref, nk_ref, nv_ref, len_ref, res_ref, gain_ref,
    k_buf, v_buf, wo_buf, wgu_buf, wt_buf, wd_buf,
    y_acc, y_stat, z_acc, z_stat, att_buf,
    gain_buf, e_buf, stream_buf, f_buf, f_own, h_send, h_buf, i_send, i_buf,
    local_sem, y_send_sem, y_recv_sem, z_send_sem, z_recv_sem, ys_send_sem, ys_recv_sem, zs_send_sem, zs_recv_sem,
    gain_send_sem, gain_recv_sem, e_send_sem, e_recv_sem, f_send_sem, f_recv_sem, h_send_sem, h_recv_sem,
    i_send_sem, i_recv_sem, small_sem,
):
    kvp, head = lax.axis_index("kvp"), lax.axis_index("head")
    y, z = kvp // NZ, lax.rem(kvp, NZ)
    x, core = head // NC, lax.rem(head, NC)
    slot = z * NY + y

    def at_yz(yy, zz):
        return (yy * NZ + zz, head)

    def at_head(hh):
        return (kvp, hh)

    def y_peer(i):
        return at_yz(lax.rem(y + jnp.where(lax.rem(i, 2) == 1, 2 - (i + 1) // 2, 2 + i // 2), NY), z)

    def z_peer(i):
        return at_yz(y, lax.rem(z + far_first(i), NZ))

    def head_peer(i):
        pair = i // NC
        dx = jnp.where(lax.rem(pair, 2) == 1, 2 - (pair + 1) // 2, 2 + pair // 2)
        return lax.rem(x + dx, NX), lax.rem(core + 1 - lax.rem(i, NC), NC)

    def each(n, body):
        for i in range(n):
            body(i)

    def every(n, body):
        def step(i, carry):
            body(i)
            return carry

        lax.fori_loop(0, n, step, 0)

    def to_heads(body, loop=False):
        def one(i):
            xx, cc = head_peer(i)
            body(xx, at_head(xx * NC + cc))

        (every if loop else each)(HEAD - 1, one)

    smalls = [
        pltpu.make_async_copy(src, dst, small_sem.at[i])
        for i, (src, dst) in enumerate(
            (
                (q_hbm, q_ref), (nk_hbm, nk_ref), (nv_hbm, nv_ref), (len_hbm, len_ref), (res_hbm, res_ref),
                (gain_hbm, gain_ref),
            )
        )
    ]
    loads = []
    for b in range(SEQS):
        loads.append(pltpu.make_async_copy(k_hbm.at[b, 0], k_buf.at[b], local_sem.at[b]))
        loads.append(pltpu.make_async_copy(v_hbm.at[b, 0], v_buf.at[b], local_sem.at[2 + b]))
    load_wo = pltpu.make_async_copy(wo_hbm, wo_buf, local_sem.at[4])
    load_wg = pltpu.make_async_copy(wg_hbm, wgu_buf.at[pl.ds(0, UNITS)], local_sem.at[5])
    load_wu = pltpu.make_async_copy(wu_hbm, wgu_buf.at[pl.ds(128, UNITS)], local_sem.at[6])
    load_wd0 = pltpu.make_async_copy(wd_hbm.at[:, pl.ds(0, D // 2)], wd_buf.at[pl.ds(0, UNITS)], local_sem.at[7])
    load_wd1 = pltpu.make_async_copy(wd_hbm.at[:, pl.ds(D // 2, D // 2)], wd_buf.at[pl.ds(128, UNITS)], local_sem.at[8])
    barrier = pltpu.get_barrier_semaphore()
    def greet(peer):
        pl.semaphore_signal(barrier, inc=1, device_id=peer, device_id_type=MESH)

    every(NZ - 1, lambda i: greet(z_peer(i)))
    to_heads(lambda xx, peer: greet(peer), True)
    every(NY - 1, lambda i: greet(y_peer(i)))

    for load in smalls[:1] + loads + smalls[1:]:
        load.start()

    def put(src, dst, send_sem, recv_sem, peer):
        pltpu.make_async_remote_copy(
            src_ref=src, dst_ref=dst, send_sem=send_sem, recv_sem=recv_sem, device_id=peer, device_id_type=MESH
        ).start()

    def drain(ref, sem):
        pltpu.make_async_copy(ref, ref, sem).wait()

    lane = lax.broadcasted_iota(jnp.int32, (1, 128), 1)
    lane16 = lax.rem(lane, GROUP)
    lane_group = lane // GROUP
    diagonal = lax.broadcasted_iota(jnp.int32, (GROUP, 128), 0) == lax.rem(
        lax.broadcasted_iota(jnp.int32, (GROUP, 128), 1), GROUP
    )
    my_half = (lane // 64) == core

    def to_row(column):
        return jnp.sum(jnp.where(diagonal, column, 0.0), axis=0, keepdims=True)

    for small in smalls + loads:
        small.wait()
    for load in (load_wg, load_wu, load_wo, load_wd0, load_wd1):
        load.start()

    gain_mine = jnp.reshape(gain_ref[...], (1, 64))
    gain_buf[head] = jnp.where(my_half, jnp.concatenate([gain_mine, gain_mine], axis=1), 0.0)

    def local_attention(b):
        q = q_ref[b]
        scores = lax.dot_general(q, k_buf[b], NT, preferred_element_type=f32) * SCALE
        positions = kvp * TOKENS + lax.broadcasted_iota(jnp.int32, (GROUP, TOKENS), 1)
        in_range = positions < len_ref[b]
        scores = jnp.where(in_range, scores, MASKED)
        first = kvp == 0
        fresh = jnp.sum(q.astype(f32) * nk_ref[b : b + 1, :].astype(f32), axis=1, keepdims=True) * SCALE
        fresh = jnp.where(first, fresh, MASKED)
        top = jnp.maximum(jnp.max(scores, axis=1, keepdims=True), fresh)
        weights = jnp.where(in_range, jnp.exp(scores - top), 0.0)
        fresh_weight = jnp.where(first, jnp.exp(fresh - top), 0.0)
        total = jnp.sum(weights, axis=1, keepdims=True) + fresh_weight
        acc = jnp.dot(weights.astype(bf16), v_buf[b], preferred_element_type=f32)
        acc = acc + fresh_weight.astype(bf16).astype(f32) * nv_ref[b : b + 1, :].astype(f32)
        return acc, to_row(top), to_row(total)

    def send_y(b, acc, top, total):
        y_acc[b, y] = acc.astype(bf16)
        y_stat[b, y] = jnp.concatenate([top, total], axis=0)

        def send(i):
            peer = y_peer(i)
            put(y_stat.at[b, y], y_stat.at[b, y], ys_send_sem.at[b], ys_recv_sem.at[b], peer)
            put(y_acc.at[b, y], y_acc.at[b, y], y_send_sem.at[b], y_recv_sem.at[b], peer)

        each(NY - 1, send)

    def send_z(b, acc, top, total):
        z_acc[b, z] = acc.astype(bf16)
        z_stat[b, z] = jnp.concatenate([top, total], axis=0)

        def send(i):
            peer = z_peer(i)
            put(z_stat.at[b, z], z_stat.at[b, z], zs_send_sem.at[b], zs_recv_sem.at[b], peer)
            put(z_acc.at[b, z], z_acc.at[b, z], z_send_sem.at[b], z_recv_sem.at[b], peer)

        each(NZ - 1, send)

    def merge(n, b, acc_buf, stat_buf, acc_sem, stat_sem, last):
        drain(stat_buf.at[b, pl.ds(0, n - 1)], stat_sem.at[b])
        tops = [stat_buf[b, s, 0:1, :] for s in range(n)]
        totals = [stat_buf[b, s, 1:2, :] for s in range(n)]
        top = tops[0]
        for t in tops[1:]:
            top = jnp.maximum(top, t)
        total = jnp.zeros((1, 128), f32)
        chosen = jnp.zeros((1, 128), f32)
        for s in range(n):
            factor = jnp.exp(tops[s] - top)
            total = total + totals[s] * factor
            chosen = jnp.where(lane_group == s, factor, chosen)
        if last:
            chosen = chosen / total
        spread = jnp.where(diagonal, chosen, 0.0).astype(bf16)
        drain(acc_buf.at[b, pl.ds(0, n - 1)], acc_sem.at[b])
        stacked = acc_buf[b].reshape(n * GROUP, HD)
        acc = jnp.dot(spread[:, : n * GROUP], stacked, preferred_element_type=f32)
        return acc, top, total

    def turn(first, last):
        def block(i, carry):
            columns = pl.ds(pl.multiple_of(i * BLOCK, BLOCK), BLOCK)
            wt_buf[columns, :] = wgu_buf[:, columns].T
            return carry

        lax.fori_loop(first, last, block, 0)

    part0 = local_attention(0)
    part1 = local_attention(1)

    pl.semaphore_wait(barrier, NZ + HEAD + NY - 3)
    send_y(0, *part0)
    send_z(1, *part1)
    to_heads(lambda xx, peer: put(gain_buf.at[head], gain_buf.at[head], gain_send_sem, gain_recv_sem, peer))


    def clear(i):
        columns = pl.ds(pl.multiple_of(i * BLOCK, BLOCK), BLOCK)
        for first in (UNITS, 128 + UNITS):
            wd_buf[first : first + 128 - UNITS, columns] = jnp.zeros((128 - UNITS, BLOCK), bf16)

    every(KVP // 2, clear)
    load_wg.wait()
    load_wu.wait()
    turn(0, 10)
    send_z(0, *merge(NY, 0, y_acc, y_stat, y_recv_sem, ys_recv_sem, False))
    send_y(1, *merge(NZ, 1, z_acc, z_stat, z_recv_sem, zs_recv_sem, False))
    att_buf[0] = merge(NZ, 0, z_acc, z_stat, z_recv_sem, zs_recv_sem, True)[0]
    att_buf[1] = merge(NY, 1, y_acc, y_stat, y_recv_sem, ys_recv_sem, True)[0]

    attended = jnp.concatenate([att_buf[:, h, :] for h in range(GROUP)], axis=1).astype(bf16)
    load_wo.wait()
    projected = jnp.dot(attended, wo_buf[...], preferred_element_type=f32)
    residual = res_ref[...].astype(f32)
    residual = jnp.where(my_half, jnp.concatenate([residual, residual], axis=1), 0.0)
    for t in range(TILES):
        e_buf[head, t] = projected[:, t * 128 : (t + 1) * 128] + jnp.where(x == t, residual, 0.0)
    to_heads(lambda xx, peer: put(e_buf.at[head], e_buf.at[head], e_send_sem, e_recv_sem, peer))
    turn(10, KVP)
    drain(gain_buf.at[pl.ds(0, HEAD - 1)], gain_recv_sem)
    gains = [gain_buf[2 * t] + gain_buf[2 * t + 1] for t in range(TILES)]
    drain(e_buf.at[pl.ds(0, HEAD - 1)], e_recv_sem)
    squares = jnp.zeros((SEQS, 128), f32)
    for t in range(TILES):
        stream = e_buf[0, t]
        for hh in range(1, HEAD):
            stream = stream + e_buf[hh, t]
        stream_buf[t] = stream
        squares = squares + stream * stream
        f_buf[slot, t] = (stream * gains[t]).astype(bf16)
    square = jnp.sum(squares, axis=1, keepdims=True)
    piece0 = square.astype(bf16).astype(f32)
    piece1 = (square - piece0).astype(bf16).astype(f32)
    piece2 = square - piece0 - piece1
    f_buf[slot, TILES] = jnp.where(
        lane == 0, piece0, jnp.where(lane == 1, piece1, jnp.where(lane == 2, piece2, 0.0))
    ).astype(bf16)

    def send_f(peer):
        put(f_buf.at[slot], f_buf.at[slot], f_send_sem, f_recv_sem.at[z], peer)

    def send_f_group(g, carry):
        zz = lax.rem(z + nth(SENT, g), NZ)
        for dy in (2, 1, 3, 0):
            send_f(at_yz(lax.rem(y + dy, NY), zz))
        return carry

    own_block = pltpu.make_async_copy(f_buf.at[slot], f_own, f_recv_sem.at[z])
    own_block.start()
    lax.fori_loop(0, NZ - 1, send_f_group, 0)
    for dy in (2, 1, 3):
        send_f(at_yz(lax.rem(y + dy, NY), z))

    def gate_up(zz, carry):
        acts, squares = carry
        for yy in range(NY):
            block = zz * NY + yy
            part = jnp.concatenate([f_buf[block, t] for t in range(TILES)], axis=1)
            columns = pl.ds(pl.multiple_of((yy * NZ + zz) * BLOCK, BLOCK), BLOCK)
            acts = acts + jnp.dot(part, wt_buf[columns, :], preferred_element_type=f32)
            squares = squares + f_buf[block, TILES].astype(f32)
        return acts, squares

    def gate_up_group(i, carry):
        zz = lax.rem(z + NZ - nth(USED, i), NZ)
        drain(f_buf.at[pl.ds(0, NY)], f_recv_sem.at[zz])
        return gate_up(zz, carry)

    carry = (jnp.zeros((SEQS, 256), f32), jnp.zeros((SEQS, 128), f32))
    acts, squares = lax.fori_loop(0, NZ, gate_up_group, carry)
    factor = lax.rsqrt(jnp.sum(squares, axis=1, keepdims=True) / D + EPSILON)
    gate = acts[:, :128] * factor
    up = acts[:, 128:] * factor
    hidden = jnp.where(lane < UNITS, gate / (1.0 + jnp.exp(-gate)) * up, 0.0)
    zeros = jnp.zeros((SEQS, 128), f32)
    hidden = jnp.concatenate(
        [jnp.concatenate([hidden, zeros], axis=1), jnp.concatenate([zeros, hidden], axis=1)], axis=0
    ).astype(bf16)

    load_wd0.wait()
    load_wd1.wait()

    def down(zz):
        for yy in range(NY // 2):
            columns = pl.ds(pl.multiple_of((yy * NZ + zz) * BLOCK, BLOCK), BLOCK)
            part = jnp.dot(hidden, wd_buf[:, columns], preferred_element_type=f32)
            for half in range(2):
                for t in range(TILES):
                    h_send[zz * NY + yy + 2 * half, t] = part[
                        SEQS * half : SEQS * (half + 1), t * 128 : (t + 1) * 128
                    ].astype(bf16)

    def send_h(yy, zz):
        put(h_send.at[zz * NY + yy], h_buf.at[slot], h_send_sem, h_recv_sem.at[z], at_yz(yy, zz))

    def down_group(g, carry):
        zz = lax.rem(z + far_first(g), NZ)
        down(zz)
        for dy in (2, 1, 3, 0):
            send_h(lax.rem(y + dy, NY), zz)
        return carry

    lax.fori_loop(0, NZ - 1, down_group, 0)
    down(z)
    for dy in (2, 1, 3):
        send_h(lax.rem(y + dy, NY), z)
    for t in range(TILES):
        h_buf[slot, t] = h_send[slot, t]

    def add_blocks(zz, sums):
        for yy in range(NY):
            sums = tuple(sums[t] + h_buf[zz * NY + yy, t].astype(f32) for t in range(TILES))
        return sums

    def add_group(i, sums):
        zz = lax.rem(z + far_first(NZ - 1 - i), NZ)
        drain(h_buf.at[pl.ds(0, NY)], h_recv_sem.at[zz])
        return add_blocks(zz, sums)

    drain(h_buf.at[pl.ds(0, NY - 1)], h_recv_sem.at[z])
    sums = add_blocks(z, tuple(jnp.zeros((SEQS, 128), f32) for _ in range(TILES)))
    sums = lax.fori_loop(1, NZ, add_group, sums)
    for t in range(TILES):
        i_send[t] = sums[t]

    to_heads(lambda xx, peer: put(i_send.at[xx], i_buf.at[head], i_send_sem, i_recv_sem, peer))
    i_buf[head] = i_send[x]
    total = stream_buf[x]
    drain(i_buf.at[pl.ds(0, HEAD - 1)], i_recv_sem)
    for hh in range(HEAD):
        total = total + i_buf[hh]
    out_ref[...] = jnp.where(core == 0, total[:, :64], total[:, 64:]).astype(bf16)

    for b in range(SEQS):
        drain(y_acc.at[b, pl.ds(0, NY - 1)], y_send_sem.at[b])
        drain(y_stat.at[b, pl.ds(0, NY - 1)], ys_send_sem.at[b])
        drain(z_acc.at[b, pl.ds(0, NZ - 1)], z_send_sem.at[b])
        drain(z_stat.at[b, pl.ds(0, NZ - 1)], zs_send_sem.at[b])
    drain(gain_buf.at[pl.ds(0, HEAD - 1)], gain_send_sem)
    drain(e_buf.at[pl.ds(0, HEAD - 1)], e_send_sem)
    drain(f_buf.at[pl.ds(0, KVP - 1)], f_send_sem)
    drain(h_buf.at[pl.ds(0, KVP - 1)], h_send_sem)
    drain(i_buf.at[pl.ds(0, HEAD - 1)], i_send_sem)


def per_device(queries, key_cache, value_cache, new_key, new_value, *rest):
    args = (queries, key_cache, value_cache, new_key.reshape(SEQS, HD), new_value.reshape(SEQS, HD)) + rest
    vmem = pl.BlockSpec(memory_space=pltpu.VMEM)
    hbm = pl.BlockSpec(memory_space=pltpu.HBM)
    dma = pltpu.SemaphoreType.DMA
    return pl.pallas_call(
        kernel,
        out_shape=pltpu.VMEM((SEQS, D // KVP // HEAD), bf16),
        in_specs=[hbm] * 12,
        out_specs=vmem,
        scratch_shapes=[
            pltpu.VMEM((SEQS, GROUP, HD), bf16),
            pltpu.VMEM((SEQS, HD), bf16),
            pltpu.VMEM((SEQS, HD), bf16),
            pltpu.SMEM((SEQS,), jnp.int32),
            pltpu.VMEM((SEQS, D // KVP // HEAD), bf16),
            pltpu.VMEM((D // KVP // HEAD,), f32),
            pltpu.VMEM((SEQS, TOKENS, HD), bf16),
            pltpu.VMEM((SEQS, TOKENS, HD), bf16),
            pltpu.VMEM((GROUP * HD, BLOCK), bf16),
            pltpu.VMEM((256, D), bf16),
            pltpu.VMEM((D, 256), bf16),
            pltpu.VMEM((256, D // 2), bf16),
            pltpu.VMEM((SEQS, NY, GROUP, HD), bf16),
            pltpu.VMEM((SEQS, NY, 2, 128), f32),
            pltpu.VMEM((SEQS, NZ, GROUP, HD), bf16),
            pltpu.VMEM((SEQS, NZ, 2, 128), f32),
            pltpu.VMEM((SEQS, GROUP, HD), f32),
            pltpu.VMEM((HEAD, 1, 128), f32),
            pltpu.VMEM((HEAD, TILES, SEQS, 128), f32),
            pltpu.VMEM((TILES, SEQS, 128), f32),
            pltpu.VMEM((KVP, TILES + 1, SEQS, 128), bf16),
            pltpu.VMEM((TILES + 1, SEQS, 128), bf16),
            pltpu.VMEM((KVP, TILES, SEQS, 128), bf16),
            pltpu.VMEM((KVP, TILES, SEQS, 128), bf16),
            pltpu.VMEM((TILES, SEQS, 128), f32),
            pltpu.VMEM((HEAD, SEQS, 128), f32),
            dma((9,)),
            dma((SEQS,)), dma((SEQS,)), dma((SEQS,)), dma((SEQS,)),
            dma((SEQS,)), dma((SEQS,)), dma((SEQS,)), dma((SEQS,)),
            dma, dma, dma, dma, dma, dma((NZ,)), dma, dma((NZ,)), dma, dma, dma((6,)),
        ],
        compiler_params=pltpu.CompilerParams(
            collective_id=0, has_side_effects=True, vmem_limit_bytes=62 * 1024 * 1024
        ),
        name="layer",
    )(*args)


def solution(mesh):
    in_specs = (
        P(None, "head", None),
        P(None, "head", "kvp", None),
        P(None, "head", "kvp", None),
        P(None, "head", None),
        P(None, "head", None),
        P(),
        P(None, ("kvp", "head")),
        P("head", "kvp"),
        P(("kvp", "head")),
        P(("kvp", "head"), None),
        P(("kvp", "head"), None),
        P(("kvp", "head"), None),
    )
    return jax.shard_map(
        per_device, mesh=mesh, in_specs=in_specs, out_specs=P(None, ("kvp", "head")), check_vma=False
    )
```

```python
import jax
import jax.numpy as jnp
from jax import lax
from jax.experimental import pallas as pl
from jax.experimental.pallas import tpu as pltpu
from jax.sharding import PartitionSpec as P

MESH = pl.DeviceIdType.MESH
NT = (((1,), (1,)), ((), ()))
f32 = jnp.float32
bf16 = jnp.bfloat16
EPSILON = 1e-05
MASKED = -1e30

NX, NY, NZ, NC = 4, 4, 8, 2
KVP, HEAD = NY * NZ, NX * NC
SEQS, GROUP, HD, TOKENS = 2, 16, 128, 512
D = 16384
BLOCK = D // KVP
TILES = BLOCK // 128
UNITS = 104
SCALE = HD**-0.5


def mod(value, n):
    return jnp.bitwise_and(value, n - 1)


def packed(offsets):
    return sum(offset << (3 * i) for i, offset in enumerate(offsets))


SENT, USED = packed((4, 1, 7, 2, 6, 3, 5)), packed((1, 7, 0, 2, 6, 4, 3, 5))
FAR_Z, NEAR_Z, FAR_Y = packed((4, 3, 5, 2, 6, 1, 7, 0)), packed((0, 7, 1, 6, 2, 5, 3, 4)), packed((2, 1, 3, 0))


def nth(offsets, i):
    return jnp.bitwise_and(lax.shift_right_logical(jnp.int32(offsets), jnp.int32(3 * i)), 7)


def kernel(
    q_hbm, k_hbm, v_hbm, nk_hbm, nv_hbm, len_hbm, res_hbm, wo_hbm, gain_hbm, wg_hbm, wu_hbm, wd_hbm,
    out_ref,
    q_ref, nk_ref, nv_ref, len_ref, res_ref, gain_ref,
    k_buf, v_buf, wo_buf, wgu_buf, wt_buf, wd_buf,
    y_acc, y_stat, z_acc, z_stat, att_buf,
    gain_buf, e_buf, stream_buf, f_buf, f_own, h_send, h_buf, i_send, i_buf,
    local_sem, y_send_sem, y_recv_sem, z_send_sem, z_recv_sem, ys_send_sem, ys_recv_sem, zs_send_sem, zs_recv_sem,
    gain_send_sem, gain_recv_sem, e_send_sem, e_recv_sem, f_send_sem, f_recv_sem, h_send_sem, h_recv_sem,
    i_send_sem, i_recv_sem, small_sem,
):
    kvp, head = lax.axis_index("kvp"), lax.axis_index("head")
    y, z = lax.shift_right_logical(kvp, 3), mod(kvp, NZ)
    x, core = lax.shift_right_logical(head, 1), mod(head, NC)
    slot = z * NY + y

    def at_yz(yy, zz):
        return (yy * NZ + zz, head)

    def at_head(hh):
        return (kvp, hh)

    def y_peer(i):
        return at_yz(mod(y + nth(FAR_Y, i), NY), z)

    def z_peer(i):
        return at_yz(y, mod(z + nth(FAR_Z, i), NZ))

    def head_peer(i):
        dx = nth(FAR_Y, i // NC if isinstance(i, int) else lax.shift_right_logical(i, 1))
        return mod(x + dx, NX), mod(core + 1 - mod(i, NC), NC)

    def each(n, body):
        for i in range(n):
            body(i)

    def every(n, body):
        def step(i, carry):
            body(i)
            return carry

        lax.fori_loop(0, n, step, 0)

    def to_heads(body, loop=False):
        def one(i):
            xx, cc = head_peer(i)
            body(xx, at_head(xx * NC + cc))

        (every if loop else each)(HEAD - 1, one)

    smalls = [
        pltpu.make_async_copy(src, dst, small_sem.at[i])
        for i, (src, dst) in enumerate(
            (
                (q_hbm, q_ref), (nk_hbm, nk_ref), (nv_hbm, nv_ref), (len_hbm, len_ref), (res_hbm, res_ref),
                (gain_hbm, gain_ref),
            )
        )
    ]
    loads = []
    for b in range(SEQS):
        loads.append(pltpu.make_async_copy(k_hbm.at[b, 0], k_buf.at[b], local_sem.at[b]))
        loads.append(pltpu.make_async_copy(v_hbm.at[b, 0], v_buf.at[b], local_sem.at[2 + b]))
    load_wo = pltpu.make_async_copy(wo_hbm, wo_buf, local_sem.at[4])
    load_wg = pltpu.make_async_copy(wg_hbm, wgu_buf.at[pl.ds(0, UNITS)], local_sem.at[5])
    load_wu = pltpu.make_async_copy(wu_hbm, wgu_buf.at[pl.ds(128, UNITS)], local_sem.at[6])
    load_wd0 = pltpu.make_async_copy(wd_hbm.at[:, pl.ds(0, D // 2)], wd_buf.at[pl.ds(0, UNITS)], local_sem.at[7])
    load_wd1 = pltpu.make_async_copy(wd_hbm.at[:, pl.ds(D // 2, D // 2)], wd_buf.at[pl.ds(128, UNITS)], local_sem.at[8])
    barrier = pltpu.get_barrier_semaphore()
    def greet(peer):
        pl.semaphore_signal(barrier, inc=1, device_id=peer, device_id_type=MESH)

    every(NZ - 1, lambda i: greet(z_peer(i)))
    to_heads(lambda xx, peer: greet(peer), True)
    every(NY - 1, lambda i: greet(y_peer(i)))

    for load in smalls[:1] + loads + smalls[1:]:
        load.start()

    def put(src, dst, send_sem, recv_sem, peer):
        pltpu.make_async_remote_copy(
            src_ref=src, dst_ref=dst, send_sem=send_sem, recv_sem=recv_sem, device_id=peer, device_id_type=MESH
        ).start()

    def drain(ref, sem):
        pltpu.make_async_copy(ref, ref, sem).wait()

    lane = lax.broadcasted_iota(jnp.int32, (1, 128), 1)
    lane_group = lane // GROUP
    diagonal = lax.broadcasted_iota(jnp.int32, (GROUP, 128), 0) == lax.rem(
        lax.broadcasted_iota(jnp.int32, (GROUP, 128), 1), GROUP
    )
    my_half = (lane // 64) == core

    def to_row(column):
        return jnp.sum(jnp.where(diagonal, column, 0.0), axis=0, keepdims=True)

    for load in smalls[:4] + loads:
        load.wait()

    def local_attention(b):
        q = q_ref[b]
        scores = lax.dot_general(q, k_buf[b], NT, preferred_element_type=f32) * SCALE
        positions = kvp * TOKENS + lax.broadcasted_iota(jnp.int32, (GROUP, TOKENS), 1)
        in_range = positions < len_ref[b]
        scores = jnp.where(in_range, scores, MASKED)
        first = kvp == 0
        fresh = jnp.sum(q.astype(f32) * nk_ref[b : b + 1, :].astype(f32), axis=1, keepdims=True) * SCALE
        fresh = jnp.where(first, fresh, MASKED)
        top = jnp.maximum(jnp.max(scores, axis=1, keepdims=True), fresh)
        weights = jnp.where(in_range, jnp.exp(scores - top), 0.0)
        fresh_weight = jnp.where(first, jnp.exp(fresh - top), 0.0)
        total = jnp.sum(weights, axis=1, keepdims=True) + fresh_weight
        acc = jnp.dot(weights.astype(bf16), v_buf[b], preferred_element_type=f32)
        acc = acc + fresh_weight.astype(bf16).astype(f32) * nv_ref[b : b + 1, :].astype(f32)
        return acc, to_row(top), to_row(total)

    def send_y(b, acc, top, total):
        y_acc[b, y] = acc.astype(bf16)
        y_stat[b, y] = jnp.concatenate([top, total], axis=0)

        def send(i):
            peer = y_peer(i)
            put(y_stat.at[b, y], y_stat.at[b, y], ys_send_sem.at[b], ys_recv_sem.at[b], peer)
            put(y_acc.at[b, y], y_acc.at[b, y], y_send_sem.at[b], y_recv_sem.at[b], peer)

        each(NY - 1, send)

    def send_z(b, acc, top, total):
        z_acc[b, z] = acc.astype(bf16)
        z_stat[b, z] = jnp.concatenate([top, total], axis=0)

        def send(i):
            peer = z_peer(i)
            put(z_stat.at[b, z], z_stat.at[b, z], zs_send_sem.at[b], zs_recv_sem.at[b], peer)
            put(z_acc.at[b, z], z_acc.at[b, z], z_send_sem.at[b], z_recv_sem.at[b], peer)

        each(NZ - 1, send)

    def merge(n, b, acc_buf, stat_buf, acc_sem, stat_sem, last):
        drain(stat_buf.at[b, pl.ds(0, n - 1)], stat_sem.at[b])
        tops = [stat_buf[b, s, 0:1, :] for s in range(n)]
        totals = [stat_buf[b, s, 1:2, :] for s in range(n)]
        top = tops[0]
        for t in tops[1:]:
            top = jnp.maximum(top, t)
        total = jnp.zeros((1, 128), f32)
        chosen = jnp.zeros((1, 128), f32)
        for s in range(n):
            factor = jnp.exp(tops[s] - top)
            total = total + totals[s] * factor
            chosen = jnp.where(lane_group == s, factor, chosen)
        if last:
            chosen = chosen / total
        spread = jnp.where(diagonal, chosen, 0.0).astype(bf16)
        drain(acc_buf.at[b, pl.ds(0, n - 1)], acc_sem.at[b])
        stacked = acc_buf[b].reshape(n * GROUP, HD)
        acc = jnp.dot(spread[:, : n * GROUP], stacked, preferred_element_type=f32)
        return acc, top, total

    def turn(first, last):
        def block(i, carry):
            columns = pl.ds(pl.multiple_of(i * BLOCK, BLOCK), BLOCK)
            wt_buf[columns, :] = wgu_buf[:, columns].T
            return carry

        lax.fori_loop(first, last, block, 0)

    part0 = local_attention(0)
    part1 = local_attention(1)

    pl.semaphore_wait(barrier, NZ + HEAD + NY - 3)
    send_y(0, *part0)
    send_z(1, *part1)
    for load in (load_wg, load_wu, load_wo, load_wd0, load_wd1):
        load.start()
    for load in smalls[4:]:
        load.wait()

    gain_mine = jnp.reshape(gain_ref[...], (1, 64))
    gain_buf[head] = jnp.where(my_half, jnp.concatenate([gain_mine, gain_mine], axis=1), 0.0)
    to_heads(lambda xx, peer: put(gain_buf.at[head], gain_buf.at[head], gain_send_sem, gain_recv_sem, peer))


    def clear(i):
        columns = pl.ds(pl.multiple_of(i * BLOCK, BLOCK), BLOCK)
        for first in (UNITS, 128 + UNITS):
            wd_buf[first : first + 128 - UNITS, columns] = jnp.zeros((128 - UNITS, BLOCK), bf16)

    send_z(0, *merge(NY, 0, y_acc, y_stat, y_recv_sem, ys_recv_sem, False))
    send_y(1, *merge(NZ, 1, z_acc, z_stat, z_recv_sem, zs_recv_sem, False))
    every(KVP // 2, clear)
    load_wg.wait()
    load_wu.wait()
    turn(0, 12)
    att_buf[0] = merge(NZ, 0, z_acc, z_stat, z_recv_sem, zs_recv_sem, True)[0]
    att_buf[1] = merge(NY, 1, y_acc, y_stat, y_recv_sem, ys_recv_sem, True)[0]

    attended = jnp.concatenate([att_buf[:, h, :] for h in range(GROUP)], axis=1).astype(bf16)
    load_wo.wait()
    projected = jnp.dot(attended, wo_buf[...], preferred_element_type=f32)
    residual = res_ref[...].astype(f32)
    residual = jnp.where(my_half, jnp.concatenate([residual, residual], axis=1), 0.0)
    for t in range(TILES):
        e_buf[head, t] = projected[:, t * 128 : (t + 1) * 128] + jnp.where(x == t, residual, 0.0)
    to_heads(lambda xx, peer: put(e_buf.at[head], e_buf.at[head], e_send_sem, e_recv_sem, peer))
    turn(12, KVP)
    drain(gain_buf.at[pl.ds(0, HEAD - 1)], gain_recv_sem)
    gains = [gain_buf[2 * t] + gain_buf[2 * t + 1] for t in range(TILES)]
    drain(e_buf.at[pl.ds(0, HEAD - 1)], e_recv_sem)
    squares = jnp.zeros((SEQS, 128), f32)
    for t in range(TILES):
        stream = e_buf[0, t]
        for hh in range(1, HEAD):
            stream = stream + e_buf[hh, t]
        stream_buf[t] = stream
        squares = squares + stream * stream
        f_buf[slot, t] = (stream * gains[t]).astype(bf16)
    square = jnp.sum(squares, axis=1, keepdims=True)
    piece0 = square.astype(bf16).astype(f32)
    piece1 = (square - piece0).astype(bf16).astype(f32)
    piece2 = square - piece0 - piece1
    f_buf[slot, TILES] = jnp.where(
        lane == 0, piece0, jnp.where(lane == 1, piece1, jnp.where(lane == 2, piece2, 0.0))
    ).astype(bf16)

    def send_f(peer):
        put(f_buf.at[slot], f_buf.at[slot], f_send_sem, f_recv_sem.at[z], peer)

    def send_f_group(g, carry):
        zz = mod(z + nth(SENT, g), NZ)
        for dy in (2, 1, 3, 0):
            send_f(at_yz(mod(y + dy, NY), zz))
        return carry

    own_block = pltpu.make_async_copy(f_buf.at[slot], f_own, f_recv_sem.at[z])
    own_block.start()
    lax.fori_loop(0, NZ - 1, send_f_group, 0)
    for dy in (2, 1, 3):
        send_f(at_yz(mod(y + dy, NY), z))

    def gate_up(zz, carry):
        acts, squares = carry
        for yy in range(NY):
            block = zz * NY + yy
            part = jnp.concatenate([f_buf[block, t] for t in range(TILES)], axis=1)
            columns = pl.ds(pl.multiple_of((yy * NZ + zz) * BLOCK, BLOCK), BLOCK)
            acts = acts + jnp.dot(part, wt_buf[columns, :], preferred_element_type=f32)
            squares = squares + f_buf[block, TILES].astype(f32)
        return acts, squares

    def gate_up_group(i, carry):
        zz = mod(z + NZ - nth(USED, i), NZ)
        drain(f_buf.at[pl.ds(0, NY)], f_recv_sem.at[zz])
        return gate_up(zz, carry)

    carry = (jnp.zeros((SEQS, 256), f32), jnp.zeros((SEQS, 128), f32))
    acts, squares = lax.fori_loop(0, NZ, gate_up_group, carry)
    factor = lax.rsqrt(jnp.sum(squares, axis=1, keepdims=True) / D + EPSILON)
    gate = acts[:, :128] * factor
    up = acts[:, 128:] * factor
    hidden = jnp.where(lane < UNITS, gate / (1.0 + jnp.exp(-gate)) * up, 0.0)
    zeros = jnp.zeros((SEQS, 128), f32)
    hidden = jnp.concatenate(
        [jnp.concatenate([hidden, zeros], axis=1), jnp.concatenate([zeros, hidden], axis=1)], axis=0
    ).astype(bf16)

    load_wd0.wait()
    load_wd1.wait()

    def down(zz):
        for yy in range(NY // 2):
            columns = pl.ds(pl.multiple_of((yy * NZ + zz) * BLOCK, BLOCK), BLOCK)
            part = jnp.dot(hidden, wd_buf[:, columns], preferred_element_type=f32)
            for half in range(2):
                for t in range(TILES):
                    h_send[zz * NY + yy + 2 * half, t] = part[
                        SEQS * half : SEQS * (half + 1), t * 128 : (t + 1) * 128
                    ].astype(bf16)

    def send_h(yy, zz):
        put(h_send.at[zz * NY + yy], h_buf.at[slot], h_send_sem, h_recv_sem.at[z], at_yz(yy, zz))

    def down_group(g, carry):
        zz = mod(z + nth(FAR_Z, g), NZ)
        down(zz)
        for dy in (2, 1, 3, 0):
            send_h(mod(y + dy, NY), zz)
        return carry

    lax.fori_loop(0, NZ - 1, down_group, 0)
    down(z)
    for dy in (2, 1, 3):
        send_h(mod(y + dy, NY), z)
    for t in range(TILES):
        h_buf[slot, t] = h_send[slot, t]
    for b in range(SEQS):
        drain(y_acc.at[b, pl.ds(0, NY - 1)], y_send_sem.at[b])
        drain(y_stat.at[b, pl.ds(0, NY - 1)], ys_send_sem.at[b])
        drain(z_acc.at[b, pl.ds(0, NZ - 1)], z_send_sem.at[b])
        drain(z_stat.at[b, pl.ds(0, NZ - 1)], zs_send_sem.at[b])
    drain(gain_buf.at[pl.ds(0, HEAD - 1)], gain_send_sem)
    drain(e_buf.at[pl.ds(0, HEAD - 1)], e_send_sem)
    drain(f_buf.at[pl.ds(0, KVP - 1)], f_send_sem)

    def add_blocks(zz, sums):
        for yy in range(NY):
            sums = tuple(sums[t] + h_buf[zz * NY + yy, t].astype(f32) for t in range(TILES))
        return sums

    def add_group(i, sums):
        zz = mod(z + nth(NEAR_Z, i), NZ)
        drain(h_buf.at[pl.ds(0, NY)], h_recv_sem.at[zz])
        return add_blocks(zz, sums)

    drain(h_buf.at[pl.ds(0, NY - 1)], h_recv_sem.at[z])
    sums = add_blocks(z, tuple(jnp.zeros((SEQS, 128), f32) for _ in range(TILES)))
    sums = lax.fori_loop(1, NZ, add_group, sums)
    for t in range(TILES):
        i_send[t] = sums[t]

    to_heads(lambda xx, peer: put(i_send.at[xx], i_buf.at[head], i_send_sem, i_recv_sem, peer))
    i_buf[head] = i_send[x]
    total = stream_buf[x]
    drain(i_buf.at[pl.ds(0, HEAD - 1)], i_recv_sem)
    for hh in range(HEAD):
        total = total + i_buf[hh]
    out_ref[...] = jnp.where(core == 0, total[:, :64], total[:, 64:]).astype(bf16)

    drain(h_buf.at[pl.ds(0, KVP - 1)], h_send_sem)
    drain(i_buf.at[pl.ds(0, HEAD - 1)], i_send_sem)


def per_device(queries, key_cache, value_cache, new_key, new_value, *rest):
    args = (queries, key_cache, value_cache, new_key.reshape(SEQS, HD), new_value.reshape(SEQS, HD)) + rest
    vmem = pl.BlockSpec(memory_space=pltpu.VMEM)
    hbm = pl.BlockSpec(memory_space=pltpu.HBM)
    dma = pltpu.SemaphoreType.DMA
    return pl.pallas_call(
        kernel,
        out_shape=pltpu.VMEM((SEQS, D // KVP // HEAD), bf16),
        in_specs=[hbm] * 12,
        out_specs=vmem,
        scratch_shapes=[
            pltpu.VMEM((SEQS, GROUP, HD), bf16),
            pltpu.VMEM((SEQS, HD), bf16),
            pltpu.VMEM((SEQS, HD), bf16),
            pltpu.SMEM((SEQS,), jnp.int32),
            pltpu.VMEM((SEQS, D // KVP // HEAD), bf16),
            pltpu.VMEM((D // KVP // HEAD,), f32),
            pltpu.VMEM((SEQS, TOKENS, HD), bf16),
            pltpu.VMEM((SEQS, TOKENS, HD), bf16),
            pltpu.VMEM((GROUP * HD, BLOCK), bf16),
            pltpu.VMEM((256, D), bf16),
            pltpu.VMEM((D, 256), bf16),
            pltpu.VMEM((256, D // 2), bf16),
            pltpu.VMEM((SEQS, NY, GROUP, HD), bf16),
            pltpu.VMEM((SEQS, NY, 2, 128), f32),
            pltpu.VMEM((SEQS, NZ, GROUP, HD), bf16),
            pltpu.VMEM((SEQS, NZ, 2, 128), f32),
            pltpu.VMEM((SEQS, GROUP, HD), f32),
            pltpu.VMEM((HEAD, 1, 128), f32),
            pltpu.VMEM((HEAD, TILES, SEQS, 128), f32),
            pltpu.VMEM((TILES, SEQS, 128), f32),
            pltpu.VMEM((KVP, TILES + 1, SEQS, 128), bf16),
            pltpu.VMEM((TILES + 1, SEQS, 128), bf16),
            pltpu.VMEM((KVP, TILES, SEQS, 128), bf16),
            pltpu.VMEM((KVP, TILES, SEQS, 128), bf16),
            pltpu.VMEM((TILES, SEQS, 128), f32),
            pltpu.VMEM((HEAD, SEQS, 128), f32),
            dma((9,)),
            dma((SEQS,)), dma((SEQS,)), dma((SEQS,)), dma((SEQS,)),
            dma((SEQS,)), dma((SEQS,)), dma((SEQS,)), dma((SEQS,)),
            dma, dma, dma, dma, dma, dma((NZ,)), dma, dma((NZ,)), dma, dma, dma((6,)),
        ],
        compiler_params=pltpu.CompilerParams(
            collective_id=0, has_side_effects=True, vmem_limit_bytes=62 * 1024 * 1024
        ),
        name="layer",
    )(*args)


def solution(mesh):
    in_specs = (
        P(None, "head", None),
        P(None, "head", "kvp", None),
        P(None, "head", "kvp", None),
        P(None, "head", None),
        P(None, "head", None),
        P(),
        P(None, ("kvp", "head")),
        P("head", "kvp"),
        P(("kvp", "head")),
        P(("kvp", "head"), None),
        P(("kvp", "head"), None),
        P(("kvp", "head"), None),
    )
    return jax.shard_map(
        per_device, mesh=mesh, in_specs=in_specs, out_specs=P(None, ("kvp", "head")), check_vma=False
    )
```

```python
import jax
import jax.numpy as jnp
from jax import lax
from jax.experimental import pallas as pl
from jax.experimental.pallas import tpu as pltpu
from jax.sharding import PartitionSpec as P

MESH = pl.DeviceIdType.MESH
NT = (((1,), (1,)), ((), ()))
f32 = jnp.float32
bf16 = jnp.bfloat16
EPSILON = 1e-05
MASKED = -1e30

NX, NY, NZ, NC = 4, 4, 8, 2
KVP, HEAD = NY * NZ, NX * NC
SEQS, GROUP, HD, TOKENS = 2, 16, 128, 512
D = 16384
BLOCK = D // KVP
TILES = BLOCK // 128
UNITS = 104
SCALE = HD**-0.5


def mod(value, n):
    return jnp.bitwise_and(value, n - 1)


def packed(offsets):
    return sum(offset << (3 * i) for i, offset in enumerate(offsets))


SENT, USED = packed((4, 1, 7, 2, 6, 3, 5)), packed((1, 7, 0, 2, 6, 4, 3, 5))
FAR_Z, NEAR_Z, FAR_Y = packed((4, 3, 5, 2, 6, 1, 7, 0)), packed((0, 7, 1, 6, 2, 5, 3, 4)), packed((2, 1, 3, 0))


def nth(offsets, i):
    return jnp.bitwise_and(lax.shift_right_logical(jnp.int32(offsets), jnp.int32(3 * i)), 7)


def kernel(
    q_hbm, k_hbm, v_hbm, nk_hbm, nv_hbm, len_hbm, res_hbm, wo_hbm, gain_hbm, wg_hbm, wu_hbm, wd_hbm,
    out_ref,
    q_ref, nk_ref, nv_ref, len_ref, res_ref, gain_ref,
    k_buf, v_buf, wo_buf, wgu_buf, wt_buf, wd_buf,
    y_acc, y_stat, z_acc, z_stat, att_buf,
    gain_buf, e_buf, stream_buf, f_buf, f_own, h_send, h_buf, i_send, i_buf,
    local_sem, y_send_sem, y_recv_sem, z_send_sem, z_recv_sem, ys_send_sem, ys_recv_sem, zs_send_sem, zs_recv_sem,
    gain_send_sem, gain_recv_sem, e_send_sem, e_recv_sem, f_send_sem, f_recv_sem, h_send_sem, h_recv_sem,
    i_send_sem, i_recv_sem, small_sem,
):
    kvp, head = lax.axis_index("kvp"), lax.axis_index("head")
    y, z = lax.shift_right_logical(kvp, 3), mod(kvp, NZ)
    x, core = lax.shift_right_logical(head, 1), mod(head, NC)
    slot = z * NY + y

    def at_yz(yy, zz):
        return (yy * NZ + zz, head)

    def at_head(hh):
        return (kvp, hh)

    def y_peer(i):
        return at_yz(mod(y + nth(FAR_Y, i), NY), z)

    def z_peer(i):
        return at_yz(y, mod(z + nth(FAR_Z, i), NZ))

    def head_peer(i):
        dx = nth(FAR_Y, i // NC if isinstance(i, int) else lax.shift_right_logical(i, 1))
        return mod(x + dx, NX), mod(core + 1 - mod(i, NC), NC)

    def each(n, body):
        for i in range(n):
            body(i)

    def every(n, body):
        def step(i, carry):
            body(i)
            return carry

        lax.fori_loop(0, n, step, 0)

    def to_heads(body, loop=False):
        def one(i):
            xx, cc = head_peer(i)
            body(xx, at_head(xx * NC + cc))

        (every if loop else each)(HEAD - 1, one)

    smalls = [
        pltpu.make_async_copy(src, dst, small_sem.at[i])
        for i, (src, dst) in enumerate(
            (
                (q_hbm, q_ref), (nk_hbm, nk_ref), (nv_hbm, nv_ref), (len_hbm, len_ref), (res_hbm, res_ref),
                (gain_hbm, gain_ref),
            )
        )
    ]
    loads = []
    for b in range(SEQS):
        loads.append(pltpu.make_async_copy(k_hbm.at[b, 0], k_buf.at[b], local_sem.at[b]))
        loads.append(pltpu.make_async_copy(v_hbm.at[b, 0], v_buf.at[b], local_sem.at[2 + b]))
    load_wo = pltpu.make_async_copy(wo_hbm, wo_buf, local_sem.at[4])
    load_wg = pltpu.make_async_copy(wg_hbm, wgu_buf.at[pl.ds(0, UNITS)], local_sem.at[5])
    load_wu = pltpu.make_async_copy(wu_hbm, wgu_buf.at[pl.ds(128, UNITS)], local_sem.at[6])
    load_wd0 = pltpu.make_async_copy(wd_hbm.at[:, pl.ds(0, D // 2)], wd_buf.at[pl.ds(0, UNITS)], local_sem.at[7])
    load_wd1 = pltpu.make_async_copy(wd_hbm.at[:, pl.ds(D // 2, D // 2)], wd_buf.at[pl.ds(128, UNITS)], local_sem.at[8])
    barrier = pltpu.get_barrier_semaphore()
    def greet(peer):
        pl.semaphore_signal(barrier, inc=1, device_id=peer, device_id_type=MESH)

    every(NZ - 1, lambda i: greet(z_peer(i)))
    to_heads(lambda xx, peer: greet(peer), True)
    every(NY - 1, lambda i: greet(y_peer(i)))

    for load in smalls[:1] + loads + smalls[1:]:
        load.start()

    def put(src, dst, send_sem, recv_sem, peer):
        pltpu.make_async_remote_copy(
            src_ref=src, dst_ref=dst, send_sem=send_sem, recv_sem=recv_sem, device_id=peer, device_id_type=MESH
        ).start()

    def drain(ref, sem):
        pltpu.make_async_copy(ref, ref, sem).wait()

    lane = lax.broadcasted_iota(jnp.int32, (1, 128), 1)
    lane_group = lane // GROUP
    diagonal = lax.broadcasted_iota(jnp.int32, (GROUP, 128), 0) == lax.rem(
        lax.broadcasted_iota(jnp.int32, (GROUP, 128), 1), GROUP
    )
    my_half = (lane // 64) == core

    def to_row(column):
        return jnp.sum(jnp.where(diagonal, column, 0.0), axis=0, keepdims=True)

    for load in smalls[:4] + loads:
        load.wait()

    def local_attention(b):
        q = q_ref[b]
        scores = lax.dot_general(q, k_buf[b], NT, preferred_element_type=f32) * SCALE
        positions = kvp * TOKENS + lax.broadcasted_iota(jnp.int32, (GROUP, TOKENS), 1)
        in_range = positions < len_ref[b]
        scores = jnp.where(in_range, scores, MASKED)
        first = kvp == 0
        fresh = jnp.sum(q.astype(f32) * nk_ref[b : b + 1, :].astype(f32), axis=1, keepdims=True) * SCALE
        fresh = jnp.where(first, fresh, MASKED)
        top = jnp.maximum(jnp.max(scores, axis=1, keepdims=True), fresh)
        weights = jnp.where(in_range, jnp.exp(scores - top), 0.0)
        fresh_weight = jnp.where(first, jnp.exp(fresh - top), 0.0)
        total = jnp.sum(weights, axis=1, keepdims=True) + fresh_weight
        acc = jnp.dot(weights.astype(bf16), v_buf[b], preferred_element_type=f32)
        acc = acc + fresh_weight.astype(bf16).astype(f32) * nv_ref[b : b + 1, :].astype(f32)
        return acc, to_row(top), to_row(total)

    def send_y(b, acc, top, total):
        y_acc[b, y] = acc.astype(bf16)
        y_stat[b, y] = jnp.concatenate([top, total], axis=0)

        def send(i):
            peer = y_peer(i)
            put(y_stat.at[b, y], y_stat.at[b, y], ys_send_sem.at[b], ys_recv_sem.at[b], peer)
            put(y_acc.at[b, y], y_acc.at[b, y], y_send_sem.at[b], y_recv_sem.at[b], peer)

        each(NY - 1, send)

    def send_z(b, acc, top, total):
        z_acc[b, z] = acc.astype(bf16)
        z_stat[b, z] = jnp.concatenate([top, total], axis=0)

        def send(i):
            peer = z_peer(i)
            put(z_stat.at[b, z], z_stat.at[b, z], zs_send_sem.at[b], zs_recv_sem.at[b], peer)
            put(z_acc.at[b, z], z_acc.at[b, z], z_send_sem.at[b], z_recv_sem.at[b], peer)

        each(NZ - 1, send)

    def merge(n, b, acc_buf, stat_buf, acc_sem, stat_sem, last):
        drain(stat_buf.at[b, pl.ds(0, n - 1)], stat_sem.at[b])
        tops = [stat_buf[b, s, 0:1, :] for s in range(n)]
        totals = [stat_buf[b, s, 1:2, :] for s in range(n)]
        top = tops[0]
        for t in tops[1:]:
            top = jnp.maximum(top, t)
        total = jnp.zeros((1, 128), f32)
        chosen = jnp.zeros((1, 128), f32)
        for s in range(n):
            factor = jnp.exp(tops[s] - top)
            total = total + totals[s] * factor
            chosen = jnp.where(lane_group == s, factor, chosen)
        if last:
            chosen = chosen / total
        spread = jnp.where(diagonal, chosen, 0.0).astype(bf16)
        drain(acc_buf.at[b, pl.ds(0, n - 1)], acc_sem.at[b])
        stacked = acc_buf[b].reshape(n * GROUP, HD)
        acc = jnp.dot(spread[:, : n * GROUP], stacked, preferred_element_type=f32)
        return acc, top, total

    def turn(first, last):
        def block(i, carry):
            columns = pl.ds(pl.multiple_of(i * BLOCK, BLOCK), BLOCK)
            wt_buf[columns, :] = wgu_buf[:, columns].T
            return carry

        lax.fori_loop(first, last, block, 0)

    part0 = local_attention(0)
    part1 = local_attention(1)

    pl.semaphore_wait(barrier, NZ + HEAD + NY - 3)
    send_y(0, *part0)
    send_z(1, *part1)
    for load in (load_wg, load_wu, load_wo, load_wd0, load_wd1):
        load.start()
    for load in smalls[4:]:
        load.wait()

    gain_mine = jnp.reshape(gain_ref[...], (1, 64))
    gain_buf[head] = jnp.where(my_half, jnp.concatenate([gain_mine, gain_mine], axis=1), 0.0)
    to_heads(lambda xx, peer: put(gain_buf.at[head], gain_buf.at[head], gain_send_sem, gain_recv_sem, peer))


    def clear(i):
        columns = pl.ds(pl.multiple_of(i * BLOCK, BLOCK), BLOCK)
        for first in (UNITS, 128 + UNITS):
            wd_buf[first : first + 128 - UNITS, columns] = jnp.zeros((128 - UNITS, BLOCK), bf16)

    send_z(0, *merge(NY, 0, y_acc, y_stat, y_recv_sem, ys_recv_sem, False))
    send_y(1, *merge(NZ, 1, z_acc, z_stat, z_recv_sem, zs_recv_sem, False))
    every(KVP // 2, clear)
    load_wg.wait()
    load_wu.wait()
    turn(0, 12)
    att_buf[0] = merge(NZ, 0, z_acc, z_stat, z_recv_sem, zs_recv_sem, True)[0]
    att_buf[1] = merge(NY, 1, y_acc, y_stat, y_recv_sem, ys_recv_sem, True)[0]

    attended = jnp.concatenate([att_buf[:, h, :] for h in range(GROUP)], axis=1).astype(bf16)
    load_wo.wait()
    projected = jnp.dot(attended, wo_buf[...], preferred_element_type=f32)
    residual = res_ref[...].astype(f32)
    residual = jnp.where(my_half, jnp.concatenate([residual, residual], axis=1), 0.0)
    for t in range(TILES):
        e_buf[head, t] = projected[:, t * 128 : (t + 1) * 128] + jnp.where(x == t, residual, 0.0)
    to_heads(lambda xx, peer: put(e_buf.at[head], e_buf.at[head], e_send_sem, e_recv_sem, peer))
    turn(12, KVP)
    drain(gain_buf.at[pl.ds(0, HEAD - 1)], gain_recv_sem)
    gains = [gain_buf[2 * t] + gain_buf[2 * t + 1] for t in range(TILES)]
    drain(e_buf.at[pl.ds(0, HEAD - 1)], e_recv_sem)
    squares = jnp.zeros((SEQS, 128), f32)
    for t in range(TILES):
        stream = e_buf[0, t]
        for hh in range(1, HEAD):
            stream = stream + e_buf[hh, t]
        stream_buf[t] = stream
        squares = squares + stream * stream
        f_buf[slot, t] = (stream * gains[t]).astype(bf16)
    square = jnp.sum(squares, axis=1, keepdims=True)
    piece0 = square.astype(bf16).astype(f32)
    piece1 = (square - piece0).astype(bf16).astype(f32)
    piece2 = square - piece0 - piece1
    f_buf[slot, TILES] = jnp.where(
        lane == 0, piece0, jnp.where(lane == 1, piece1, jnp.where(lane == 2, piece2, 0.0))
    ).astype(bf16)

    def send_f(peer, far):
        put(f_buf.at[slot], f_buf.at[slot], f_send_sem, f_recv_sem.at[2 * z + far], peer)

    def send_f_group(g, carry):
        zz = mod(z + nth(SENT, g), NZ)
        for dy in (2, 1, 3, 0):
            send_f(at_yz(mod(y + dy, NY), zz), dy // 2)
        return carry

    own_block = pltpu.make_async_copy(f_buf.at[slot], f_own, f_recv_sem.at[2 * z])
    own_block.start()
    lax.fori_loop(0, NZ - 1, send_f_group, 0)
    for dy in (2, 1, 3):
        send_f(at_yz(mod(y + dy, NY), z), dy // 2)

    def gate_up(zz, carry):
        acts, squares = carry
        for dy in range(NY):
            if dy % 2 == 0:
                drain(f_buf.at[pl.ds(0, 2)], f_recv_sem.at[2 * zz + dy // 2])
            yy = mod(y + NY - dy, NY)
            block = zz * NY + yy
            part = jnp.concatenate([f_buf[block, t] for t in range(TILES)], axis=1)
            columns = pl.ds(pl.multiple_of((yy * NZ + zz) * BLOCK, BLOCK), BLOCK)
            acts = acts + jnp.dot(part, wt_buf[columns, :], preferred_element_type=f32)
            squares = squares + f_buf[block, TILES].astype(f32)
        return acts, squares

    def gate_up_group(i, carry):
        zz = mod(z + NZ - nth(USED, i), NZ)
        return gate_up(zz, carry)

    carry = (jnp.zeros((SEQS, 256), f32), jnp.zeros((SEQS, 128), f32))
    acts, squares = lax.fori_loop(0, NZ, gate_up_group, carry)
    factor = lax.rsqrt(jnp.sum(squares, axis=1, keepdims=True) / D + EPSILON)
    gate = acts[:, :128] * factor
    up = acts[:, 128:] * factor
    hidden = jnp.where(lane < UNITS, gate / (1.0 + jnp.exp(-gate)) * up, 0.0)
    zeros = jnp.zeros((SEQS, 128), f32)
    hidden = jnp.concatenate(
        [jnp.concatenate([hidden, zeros], axis=1), jnp.concatenate([zeros, hidden], axis=1)], axis=0
    ).astype(bf16)

    load_wd0.wait()
    load_wd1.wait()

    def down(zz):
        for yy in range(NY // 2):
            columns = pl.ds(pl.multiple_of((yy * NZ + zz) * BLOCK, BLOCK), BLOCK)
            part = jnp.dot(hidden, wd_buf[:, columns], preferred_element_type=f32)
            for half in range(2):
                for t in range(TILES):
                    h_send[zz * NY + yy + 2 * half, t] = part[
                        SEQS * half : SEQS * (half + 1), t * 128 : (t + 1) * 128
                    ].astype(bf16)

    def send_h(yy, zz):
        put(h_send.at[zz * NY + yy], h_buf.at[slot], h_send_sem, h_recv_sem.at[z], at_yz(yy, zz))

    def down_group(g, carry):
        zz = mod(z + nth(FAR_Z, g), NZ)
        down(zz)
        for dy in (2, 1, 3, 0):
            send_h(mod(y + dy, NY), zz)
        return carry

    lax.fori_loop(0, NZ - 1, down_group, 0)
    down(z)
    for dy in (2, 1, 3):
        send_h(mod(y + dy, NY), z)
    for t in range(TILES):
        h_buf[slot, t] = h_send[slot, t]
    for b in range(SEQS):
        drain(y_acc.at[b, pl.ds(0, NY - 1)], y_send_sem.at[b])
        drain(y_stat.at[b, pl.ds(0, NY - 1)], ys_send_sem.at[b])
        drain(z_acc.at[b, pl.ds(0, NZ - 1)], z_send_sem.at[b])
        drain(z_stat.at[b, pl.ds(0, NZ - 1)], zs_send_sem.at[b])
    drain(gain_buf.at[pl.ds(0, HEAD - 1)], gain_send_sem)
    drain(e_buf.at[pl.ds(0, HEAD - 1)], e_send_sem)
    drain(f_buf.at[pl.ds(0, KVP - 1)], f_send_sem)

    def add_blocks(zz, sums):
        for yy in range(NY):
            sums = tuple(sums[t] + h_buf[zz * NY + yy, t].astype(f32) for t in range(TILES))
        return sums

    def add_group(i, sums):
        zz = mod(z + nth(NEAR_Z, i), NZ)
        drain(h_buf.at[pl.ds(0, NY)], h_recv_sem.at[zz])
        return add_blocks(zz, sums)

    drain(h_buf.at[pl.ds(0, NY - 1)], h_recv_sem.at[z])
    sums = add_blocks(z, tuple(jnp.zeros((SEQS, 128), f32) for _ in range(TILES)))
    sums = lax.fori_loop(1, NZ, add_group, sums)
    for t in range(TILES):
        i_send[t] = sums[t]

    to_heads(lambda xx, peer: put(i_send.at[xx], i_buf.at[head], i_send_sem, i_recv_sem, peer))
    i_buf[head] = i_send[x]
    total = stream_buf[x]
    drain(i_buf.at[pl.ds(0, HEAD - 1)], i_recv_sem)
    for hh in range(HEAD):
        total = total + i_buf[hh]
    out_ref[...] = jnp.where(core == 0, total[:, :64], total[:, 64:]).astype(bf16)

    drain(h_buf.at[pl.ds(0, KVP - 1)], h_send_sem)
    drain(i_buf.at[pl.ds(0, HEAD - 1)], i_send_sem)


def per_device(queries, key_cache, value_cache, new_key, new_value, *rest):
    args = (queries, key_cache, value_cache, new_key.reshape(SEQS, HD), new_value.reshape(SEQS, HD)) + rest
    vmem = pl.BlockSpec(memory_space=pltpu.VMEM)
    hbm = pl.BlockSpec(memory_space=pltpu.HBM)
    dma = pltpu.SemaphoreType.DMA
    return pl.pallas_call(
        kernel,
        out_shape=pltpu.VMEM((SEQS, D // KVP // HEAD), bf16),
        in_specs=[hbm] * 12,
        out_specs=vmem,
        scratch_shapes=[
            pltpu.VMEM((SEQS, GROUP, HD), bf16),
            pltpu.VMEM((SEQS, HD), bf16),
            pltpu.VMEM((SEQS, HD), bf16),
            pltpu.SMEM((SEQS,), jnp.int32),
            pltpu.VMEM((SEQS, D // KVP // HEAD), bf16),
            pltpu.VMEM((D // KVP // HEAD,), f32),
            pltpu.VMEM((SEQS, TOKENS, HD), bf16),
            pltpu.VMEM((SEQS, TOKENS, HD), bf16),
            pltpu.VMEM((GROUP * HD, BLOCK), bf16),
            pltpu.VMEM((256, D), bf16),
            pltpu.VMEM((D, 256), bf16),
            pltpu.VMEM((256, D // 2), bf16),
            pltpu.VMEM((SEQS, NY, GROUP, HD), bf16),
            pltpu.VMEM((SEQS, NY, 2, 128), f32),
            pltpu.VMEM((SEQS, NZ, GROUP, HD), bf16),
            pltpu.VMEM((SEQS, NZ, 2, 128), f32),
            pltpu.VMEM((SEQS, GROUP, HD), f32),
            pltpu.VMEM((HEAD, 1, 128), f32),
            pltpu.VMEM((HEAD, TILES, SEQS, 128), f32),
            pltpu.VMEM((TILES, SEQS, 128), f32),
            pltpu.VMEM((KVP, TILES + 1, SEQS, 128), bf16),
            pltpu.VMEM((TILES + 1, SEQS, 128), bf16),
            pltpu.VMEM((KVP, TILES, SEQS, 128), bf16),
            pltpu.VMEM((KVP, TILES, SEQS, 128), bf16),
            pltpu.VMEM((TILES, SEQS, 128), f32),
            pltpu.VMEM((HEAD, SEQS, 128), f32),
            dma((9,)),
            dma((SEQS,)), dma((SEQS,)), dma((SEQS,)), dma((SEQS,)),
            dma((SEQS,)), dma((SEQS,)), dma((SEQS,)), dma((SEQS,)),
            dma, dma, dma, dma, dma, dma((2 * NZ,)), dma, dma((NZ,)), dma, dma, dma((6,)),
        ],
        compiler_params=pltpu.CompilerParams(
            collective_id=0, has_side_effects=True, vmem_limit_bytes=62 * 1024 * 1024
        ),
        name="layer",
    )(*args)


def solution(mesh):
    in_specs = (
        P(None, "head", None),
        P(None, "head", "kvp", None),
        P(None, "head", "kvp", None),
        P(None, "head", None),
        P(None, "head", None),
        P(),
        P(None, ("kvp", "head")),
        P("head", "kvp"),
        P(("kvp", "head")),
        P(("kvp", "head"), None),
        P(("kvp", "head"), None),
        P(("kvp", "head"), None),
    )
    return jax.shard_map(
        per_device, mesh=mesh, in_specs=in_specs, out_specs=P(None, ("kvp", "head")), check_vma=False
    )
```
